128 devices in a mesh: exp: 4 (over x), patch: 32 (over z, y, core).
Axes of the slice: x: 4, y: 4, z: 4, core: 2. Of those that a mesh axis runs over, the one named last changes fastest.
Arguments:
- images: bfloat16 [1024, 512, 512], P(('exp', 'patch')), may hold values from -6 to 6
- variance: bfloat16 [1024, 512, 512], P(('exp', 'patch')), may hold values from 0.5 to 8
- kernel_x: bfloat16 [16, 21], replicated, may hold values from -1.25 to 1.25
- kernel_y: bfloat16 [16, 21], replicated, may hold values from -1.25 to 1.25
- coef: float32 [1024, 16], P(('exp', 'patch')), may hold values from -1.5 to 1.5
- exposure_filter: int32 [1024], P(('exp', 'patch')), may hold values from 0 to 5
- block_patch: int32 [1024, 16], P(('exp', 'patch')), may hold values from 0 to 511, as said below
- patch_home: int32 [128], replicated, may hold values from 0 to 127, as said below
Outputs:
- coadd: float32 [128, 6, 256, 256], P('patch', None, 'exp')
The draws below stay inside these ranges and needn't reach their ends.
Inputs may be any that keep to these rules, and one draw needn't show every extreme that they name: `block_patch`: entry 4 p + q names quadrant q of patch p. Of the 128 blocks of the cells of one device, at most 6 go to patches with the same patch_home // 4, and on every device exactly 6 go to one such value. `patch_home`: each number once.
All inputs are finite; a program needn't handle non-finite values.
Results may differ from the reference program's by a relative error of at most 0.0052.
Values may be sent and summed in bfloat16 or wider, within the bound.
A program may use at most 192 MiB of HBM per device.

```python
import math
import jax
import jax.numpy as jnp
from jax import lax

CELL = 512
TAPS = 21
BASIS = 16
FILTERS = 6
CELL_DEV = 8
PATCH_DEV = 4
CELLS = 1024
PATCHES = 128
CAP = 6


def shared_home(key):
    return jax.random.permutation(jax.random.fold_in(key, 101), PATCHES).astype(jnp.int32)


def draw_patch_home(key, part):
    home_table = shared_home(key)
    return home_table


def draw_block_patch(key, part):
    home_table = shared_home(key)
    key = jax.random.fold_in(key, 5)
    key_list = jax.random.split(key, 7)
    inverse = jnp.argsort(home_table).astype(jnp.int32)
    devices_count = CELLS // CELL_DEV
    owners_count = PATCHES // PATCH_DEV
    per_device = 16 * CELL_DEV
    first_pick = jax.random.randint(key_list[0], (devices_count,), 0, owners_count)
    second_pick = jax.random.randint(key_list[1], (devices_count,), 0, owners_count)
    owner_order = jax.random.permutation(key_list[2], owners_count).astype(jnp.int32)
    hottest = owner_order[jnp.minimum(first_pick, second_pick)]
    offsets = jax.random.randint(key_list[3], (devices_count,), 0, owners_count - 1)
    others = jnp.arange(per_device - CAP, dtype=jnp.int32)
    spread = (hottest[:, None] + 1 + (others[None, :] + offsets[:, None]) % (owners_count - 1)) % owners_count
    listing = jnp.concatenate([jnp.broadcast_to(hottest[:, None], (devices_count, CAP)), spread], axis=1)
    shuffles = jax.vmap(lambda subkey: jax.random.permutation(subkey, per_device))(jax.random.split(key_list[4], devices_count))
    listing = jnp.take_along_axis(listing, shuffles.astype(jnp.int32), axis=1)
    local_slot = jax.random.randint(key_list[5], (devices_count, per_device), 0, PATCH_DEV)
    quadrant = jax.random.randint(key_list[6], (devices_count, per_device), 0, 4)
    patch_index = inverse[listing * PATCH_DEV + local_slot]
    return (patch_index * 4 + quadrant).reshape(CELLS, 16).astype(jnp.int32)


def set_ends(result, key, low, high):
    longest = result.shape.index(max(result.shape))
    spots = []
    for shift in (0, 1):
        where = [jax.random.randint(jax.random.fold_in(key, axis), (), 0, length) for axis, length in enumerate(result.shape)]
        where[longest] = (where[longest] + shift) % result.shape[longest]
        spots.append(tuple(where))
    return result.at[spots[0]].set(low).at[spots[1]].set(high)


def block_levels(stream_key, shape, shards, smallest, high):
    def one(position, blocks):
        steps = jax.random.uniform(jax.random.fold_in(jax.random.fold_in(stream_key, 6), position), (blocks,), jnp.float32, smallest / len(shards), high / len(shards))
        return jnp.repeat(jnp.exp(steps), shape[position] // blocks).reshape((-1,) + (1,) * (len(shape) - position - 1))

    level = one(*shards[0])
    for cut in shards[1:]:
        level = level * one(*cut)
    return level


def gaussian(stream_key, extent, width, bound, pieces=(), kind=jnp.bfloat16):
    loudness = block_levels(stream_key, extent, pieces, -0.22, 0.18) if pieces else 1.0
    array = jax.random.normal(stream_key, extent, jnp.float32) * width * loudness
    return jnp.minimum(jnp.maximum(array, -bound), bound).astype(kind)


def setup_inputs(seed: int = 0) -> dict:
    key_of = jax.random.split(jax.random.key(seed), 9)
    images = gaussian(key_of[0], (CELLS, CELL, CELL), 1.0, 6.0, ((0, 128),))
    variance = jnp.clip(jnp.exp(math.log(8.0) - 2.7725887 * jax.random.uniform(key_of[1], (CELLS, CELL, CELL), jnp.float32) ** block_levels(key_of[1], (CELLS, CELL, CELL), ((0, 128),), -0.2, 0.2)), 0.5, 8.0).astype(jnp.bfloat16)
    kernel_x = gaussian(key_of[2], (BASIS, TAPS), TAPS ** -0.5, 1.25)
    kernel_y = gaussian(key_of[3], (BASIS, TAPS), TAPS ** -0.5, 1.25)
    coef = gaussian(key_of[4], (CELLS, BASIS), BASIS ** -0.5, 1.5, ((0, 128),), jnp.float32)
    exposure_filter = set_ends(jax.random.randint(key_of[5], (CELLS,), 0, FILTERS), jax.random.fold_in(key_of[5], 1), 0, FILTERS - 1).astype(jnp.int32)
    block_patch = draw_block_patch(jax.random.fold_in(key_of[8], 71), 0)
    patch_home = draw_patch_home(jax.random.fold_in(key_of[8], 71), 0)
    return dict(images=images, variance=variance, kernel_x=kernel_x, kernel_y=kernel_y, coef=coef, exposure_filter=exposure_filter, block_patch=block_patch, patch_home=patch_home)


HIGHEST = lax.Precision.HIGHEST


def match_cell(operands, kernel_x, kernel_y):
    image_cell, variance_cell, coef_cell = operands
    margin = TAPS // 2
    lifted = image_cell.astype(jnp.float32)[None, None]
    row_kernel = kernel_x.astype(jnp.float32)[:, None, None, :]
    row_pass = lax.conv_general_dilated(lifted, row_kernel, (1, 1), ((0, 0), (margin, margin)), precision=HIGHEST)
    row_pass = lax.optimization_barrier(row_pass.astype(jnp.bfloat16)).astype(jnp.float32)
    scaled = lax.optimization_barrier((coef_cell[:, None] * kernel_y.astype(jnp.float32)).astype(jnp.bfloat16))
    column_kernel = scaled.astype(jnp.float32)[None, :, :, None]
    matched = lax.conv_general_dilated(row_pass, column_kernel, (1, 1), ((margin, margin), (0, 0)), precision=HIGHEST)[0, 0]
    weight = 1.0 / variance_cell.astype(jnp.float32)
    return (matched * weight).astype(jnp.bfloat16), weight.astype(jnp.bfloat16)


def reference(images, variance, kernel_x, kernel_y, coef, exposure_filter, block_patch, patch_home):
    flux_cells, weight_cells = lax.map(lambda operands: match_cell(operands, kernel_x, kernel_y), (images, variance, coef))
    block_side = CELL // 4

    def to_blocks(field_cells):
        shaped = field_cells.reshape(CELLS, 4, block_side, 4, block_side).transpose(0, 1, 3, 2, 4)
        return shaped.reshape(CELLS * 16, block_side, block_side).astype(jnp.float32)

    targets = block_patch.reshape(-1)
    patch_index = targets // 4
    quadrant = targets % 4
    band_index = jnp.repeat(exposure_filter, 16)
    plane_index = (patch_home[patch_index] * 4 + quadrant) * FILTERS + band_index
    plane_count = PATCHES * 4 * FILTERS
    numerator = jnp.zeros((plane_count, block_side, block_side), jnp.float32).at[plane_index].add(to_blocks(flux_cells))
    denominator = jnp.zeros((plane_count, block_side, block_side), jnp.float32).at[plane_index].add(to_blocks(weight_cells))

    def assemble(planes):
        shaped = planes.reshape(PATCHES, 2, 2, FILTERS, block_side, block_side).transpose(0, 3, 1, 4, 2, 5)
        return shaped.reshape(PATCHES, FILTERS, 2 * block_side, 2 * block_side)

    return assemble(numerator) / jnp.maximum(assemble(denominator), 1.0)
```

```python
import functools

import jax
import jax.numpy as jnp
from jax import lax
from jax.experimental import pallas as pl
from jax.experimental.pallas import tpu as pltpu
from jax.sharding import PartitionSpec as P

FILTERS = 6
TAPS = 21
BASIS = 16
CHUNKS = 4
CAP = 6
BF16 = jnp.bfloat16
F32 = jnp.float32


def swap_groups(v):
    sub = lax.broadcasted_iota(jnp.int32, v.shape, v.ndim - 2)
    grp = lax.broadcasted_iota(jnp.int32, v.shape, v.ndim - 1) // 16
    ax_s, ax_l = v.ndim - 2, v.ndim - 1
    for s in (1, 2, 4):
        low = (sub & s) == 0
        same = low == ((grp & s) == 0)
        down = pltpu.roll(pltpu.roll(v, 16 * s, ax_l), 8 - s, ax_s)
        if s == 4:
            v = jnp.where(same, v, down)
        else:
            up = pltpu.roll(pltpu.roll(v, 128 - 16 * s, ax_l), s, ax_s)
            v = jnp.where(same, v, jnp.where(low, down, up))
    return v


def to_tiles(rows):
    v = swap_groups(rows.reshape(2, 2, 8, 128))
    return jnp.concatenate([v[:, 0], v[:, 1]], axis=-1)


def match_kernel(dest, img, var, coef, bx, ry, *rest):
    outs, (src, wts, rolled, acc, blocks, sems) = rest[:CHUNKS], rest[CHUNKS:]
    cell = pl.program_id(0)
    cells = pl.num_programs(0)
    slot = lax.rem(cell, 2)
    tiles = src.shape[1]

    scaled = (coef[0] * ry[...]).astype(BF16)
    core = jnp.dot(bx[...], scaled, preferred_element_type=F32)
    side = jnp.zeros((48, 256), F32)
    wide = jnp.concatenate([side, core, side], axis=1)
    for r in range(8):
        turned = wide if r == 0 else pltpu.roll(wide, 1024 - 16 * r, 1)
        rolled[r] = turned.astype(BF16)
    for jy in range(48):
        start = 47 - jy
        r, base = start % 8, start // 8 * 128
        for dx in range(3):
            wts[jy // 16, pl.ds(dx * 256 + jy % 16 * 16, 16), :] = rolled[
                r, pl.ds(dx * 16, 16), pl.ds(base, 256)
            ]

    zero_rows = jnp.zeros((2, 16, 768), BF16)
    src[:, pl.ds(0, 16), :] = zero_rows
    src[:, pl.ds(tiles - 16, 16), :] = zero_rows
    sub = lax.broadcasted_iota(jnp.int32, (2, 8, 256), 1)

    def tile_rows(t, _):
        row0 = pl.multiple_of(t * 32, 32)
        strips = [
            to_tiles(img[0, pl.ds(row0, 32), pl.ds(128 * b, 128)].astype(F32)) for b in range(4)
        ]
        zero = jnp.zeros((2, 8, 256), F32)
        before = [zero] + strips[:-1]
        after = strips[1:] + [zero]
        left = [
            pltpu.roll(jnp.where(sub == 7, p, c), 1, 1) for p, c in zip(before, strips, strict=True)
        ]
        right = [
            pltpu.roll(jnp.where(sub == 0, n, c), 7, 1) for n, c in zip(after, strips, strict=True)
        ]
        dst = pl.multiple_of(16 + t * 32, 16)
        for pair in range(2):
            for dx, group in enumerate((left, strips, right)):
                both = jnp.concatenate([group[2 * pair], group[2 * pair + 1]], axis=1)
                src[pair, pl.ds(dst, 32), pl.ds(dx * 256, 256)] = both.reshape(32, 256).astype(BF16)
        return 0

    lax.fori_loop(0, 16, tile_rows, 0)

    def conv(step, _):
        pair, row0 = step // 2, pl.multiple_of(lax.rem(step, 2) * 256, 256)
        total = jnp.dot(src[pair, pl.ds(row0, 256), :], wts[0], preferred_element_type=F32)
        for dy in range(1, 3):
            total += jnp.dot(
                src[pair, pl.ds(pl.multiple_of(row0 + 16 * dy, 16), 256), :],
                wts[dy],
                preferred_element_type=F32,
            )
        acc[pair, pl.ds(row0, 256), :] = total
        return 0

    lax.fori_loop(0, 4, conv, 0)

    def block_copy(c, b, where, sl):
        return pltpu.make_async_copy(blocks.at[sl, c, b], outs[c].at[where], sems.at[sl])

    def drain(sl, count):
        def one(i, _):
            block_copy(0, 0, 0, sl).wait()
            return 0

        lax.fori_loop(0, count, one, 0)

    @pl.when(cell >= 2)
    def _():
        drain(slot, 16 * CHUNKS)

    def finish(step, _):
        by, c = step // 4, lax.rem(step, 4)
        ty = [by * 8 + c, by * 8 + 4 + c]
        for b in range(4):
            rows = jnp.concatenate(
                [
                    var[0, pl.ds(pl.multiple_of(t * 16, 16), 16), pl.ds(128 * b, 128)].astype(F32)
                    for t in ty
                ],
                axis=0,
            )
            weight = 1.0 / to_tiles(rows).reshape(16, 256)
            got = jnp.concatenate(
                [
                    acc[b // 2, pl.ds(pl.multiple_of(t * 16 + b % 2 * 8, 8), 8), :]
                    for t in ty
                ],
                axis=0,
            )
            blocks[slot, c, by * 4 + b, 0] = (got * weight).astype(BF16)
            blocks[slot, c, by * 4 + b, 1] = weight.astype(BF16)
        return 0

    lax.fori_loop(0, 16, finish, 0)

    def send(b, _):
        where = dest[cell * 16 + b]
        for c in range(CHUNKS):
            block_copy(c, b, where, slot).start()
        return 0

    lax.fori_loop(0, 16, send, 0)

    @pl.when(cell == cells - 1)
    def _():
        real = cells * 16
        fill = outs[0].shape[0] - real

        def pad(i, _):
            where = dest[real + i]
            for c in range(CHUNKS):
                block_copy(c, 0, where, slot).start()
            return 0

        lax.fori_loop(0, fill, pad, 0)
        drain(slot, (16 + fill) * CHUNKS)
        drain(1 - slot, 16 * CHUNKS)


def match_cells(dest, images, variance, coef_rows, band_x, rows_y, slots):
    cells = images.shape[0]
    out = jax.ShapeDtypeStruct((slots, 2, 16, 256), BF16)
    grid_spec = pltpu.PrefetchScalarGridSpec(
        num_scalar_prefetch=1,
        grid=(cells,),
        in_specs=[
            pl.BlockSpec((1, 512, 512), lambda i, d: (i, 0, 0)),
            pl.BlockSpec((1, 512, 512), lambda i, d: (i, 0, 0)),
            pl.BlockSpec((1, 256, 1), lambda i, d: (i, 0, 0)),
            pl.BlockSpec((48, 256), lambda i, d: (0, 0)),
            pl.BlockSpec((256, 512), lambda i, d: (0, 0)),
        ],
        out_specs=[pl.BlockSpec(memory_space=pl.ANY)] * CHUNKS,
        scratch_shapes=[
            pltpu.VMEM((2, 34 * 16, 768), BF16),
            pltpu.VMEM((3, 768, 256), BF16),
            pltpu.VMEM((8, 48, 1024), BF16),
            pltpu.VMEM((2, 512, 256), F32),
            pltpu.VMEM((2, CHUNKS, 16, 2, 16, 256), BF16),
            pltpu.SemaphoreType.DMA((2,)),
        ],
    )
    return pl.pallas_call(
        match_kernel,
        out_shape=[out] * CHUNKS,
        grid_spec=grid_spec,
        compiler_params=pltpu.CompilerParams(vmem_limit_bytes=48 * 2**20),
        name="match_cells",
    )(dest, images, variance, coef_rows, band_x, rows_y)


def add_kernel(code, got, out, acc):
    step = pl.program_id(0)
    per = got.shape[0]

    @pl.when(step == 0)
    def _():
        acc[...] = jnp.zeros_like(acc)

    def one(i, _):
        plane = code[step * per + i]
        acc[plane] += got[i].astype(F32)
        return 0

    lax.fori_loop(0, per, one, 0, unroll=2)

    @pl.when(step == pl.num_programs(0) - 1)
    def _():
        def put(p, _):
            for qy in range(2):
                both = acc[qy * 48 + p]
                for half in range(2):
                    part = both[:, 8 * half : 8 * half + 8, :]
                    out[2 * qy + half, p] = part.reshape(16, 256).astype(BF16)
            return 0

        lax.fori_loop(0, 48, put, 0)


def add_slots(code, got):
    slots = got.shape[0]
    per = slots // 6
    return pl.pallas_call(
        add_kernel,
        out_shape=jax.ShapeDtypeStruct((4, 48, 16, 256), BF16),
        grid_spec=pltpu.PrefetchScalarGridSpec(
            num_scalar_prefetch=1,
            grid=(6,),
            in_specs=[pl.BlockSpec((per, 2, 16, 256), lambda i, d: (i, 0, 0, 0))],
            out_specs=pl.BlockSpec((4, 48, 16, 256), lambda i, d: (0, 0, 0, 0)),
            scratch_shapes=[pltpu.VMEM((97, 2, 16, 256), F32)],
        ),
        compiler_params=pltpu.CompilerParams(vmem_limit_bytes=48 * 2**20),
        cost_estimate=pl.CostEstimate(flops=6000000, bytes_accessed=6000000, transcendentals=0),
        name="add_slots",
    )(code, got)


def ratio_kernel(*refs):
    ins, out = refs[:-1], refs[-1]

    def one(i, _):
        f, qx = i // 2, lax.rem(i, 2)
        for c, part in enumerate(ins):
            total = part[0, qx * 6 + f].astype(F32)
            for e in range(1, 4):
                total += part[e, qx * 6 + f].astype(F32)
            value = total[:8] / jnp.maximum(total[8:], 1.0)
            both = jnp.stack([value[:, :128], value[:, 128:]])
            cols = pl.ds(pl.multiple_of(qx * 128, 128), 128)
            out[0, f, pl.ds(16 * c, 16), cols] = swap_groups(both).reshape(16, 128)
        return 0

    lax.fori_loop(0, 12, one, 0)


def ratio(parts):
    patches = parts[0].shape[1] // 12
    return pl.pallas_call(
        ratio_kernel,
        grid=(patches,),
        out_shape=jax.ShapeDtypeStruct((patches, FILTERS, 64, 256), F32),
        in_specs=[pl.BlockSpec((4, 12, 16, 256), lambda i: (0, i, 0, 0))] * CHUNKS,
        out_specs=pl.BlockSpec((1, FILTERS, 64, 256), lambda i: (i, 0, 0, 0)),
        compiler_params=pltpu.CompilerParams(vmem_limit_bytes=48 * 2**20),
        name="ratio",
    )(*parts)


def tap_tables(kernel_x, kernel_y):
    jx = jnp.arange(48)[:, None]
    ix = jnp.arange(16)[None, :]
    pick = ((jx - ix - 6)[None] == jnp.arange(TAPS)[:, None, None]).astype(BF16)
    band_x = jnp.einsum("kt,tji->jki", kernel_x, pick, preferred_element_type=F32)
    band_x = band_x.astype(BF16).reshape(48, BASIS * 16)
    m = jnp.arange(32) + 16
    pick_y = ((41 - m)[None, :] == jnp.arange(TAPS)[:, None]).astype(BF16)
    taps_y = jnp.dot(kernel_y, pick_y, preferred_element_type=F32)
    eye = jnp.arange(16)[:, None] == jnp.arange(16)[None, :]
    rows_y = jnp.where(eye[None, :, None, :], taps_y[:, None, :, None], 0.0)
    return band_x, rows_y.reshape(BASIS * 16, 512)


def on_device(images, variance, kernel_x, kernel_y, coef, exposure_filter, block_patch, patch_home):
    cell_count = images.shape[0]
    owner_count = lax.axis_size("patch")
    patches_local = patch_home.shape[0] // owner_count
    block_count = cell_count * 16
    slots = owner_count * CAP

    targets = block_patch.reshape(-1)
    patch_index = targets // 4
    quadrant = targets % 4
    home_slot = jnp.sum(
        jnp.where(
            patch_index[:, None] == jnp.arange(patch_home.shape[0])[None, :], patch_home[None, :], 0
        ),
        axis=1,
    )
    owner_index = home_slot // patches_local
    local_patch = home_slot % patches_local
    band_index = jnp.repeat(exposure_filter, 16)
    order = jnp.arange(block_count)
    earlier = order[None, :] < order[:, None]
    rank = jnp.sum((owner_index[:, None] == owner_index[None, :]) & earlier, axis=1)
    dest = owner_index * CAP + rank
    slot_ids = jnp.arange(slots)
    hits = dest[None, :] == slot_ids[:, None]
    code = (
        (quadrant // 2) * 48 + (local_patch * 2 + quadrant % 2) * FILTERS + band_index
    )
    slot_code = jnp.min(jnp.where(hits, code[None, :], 96), axis=1)
    empty = slot_code == 96
    empty_rank = jnp.sum(empty[None, :] & (slot_ids[None, :] < slot_ids[:, None]), axis=1)
    place = jnp.arange(slots - block_count)
    spare = jnp.sum(
        jnp.where(
            empty[None, :] & (empty_rank[None, :] == place[:, None]), slot_ids[None, :], 0
        ),
        axis=1,
    )
    dest_all = jnp.concatenate([dest, spare]).astype(jnp.int32)
    got_code = lax.all_to_all(
        slot_code.astype(BF16).reshape(owner_count, CAP), "patch", 0, 0, tiled=True
    )
    got_code = got_code.reshape(-1).astype(jnp.int32)

    band_x, rows_y = tap_tables(kernel_x, kernel_y)
    coef_rows = jnp.repeat(coef, 16, axis=1)[:, :, None]
    sent = match_cells(dest_all, images, variance, coef_rows, band_x, rows_y, slots)

    shares = []
    for part in sent:
        got = lax.all_to_all(part, "patch", 0, 0, tiled=True)
        planes = add_slots(got_code, got)
        shares.append(lax.all_to_all(planes, "exp", 0, 0, tiled=True))
    return ratio(shares)


def solution(mesh):
    return jax.shard_map(
        on_device,
        mesh=mesh,
        in_specs=(
            P(("exp", "patch"), None, None),
            P(("exp", "patch"), None, None),
            P(),
            P(),
            P(("exp", "patch"), None),
            P(("exp", "patch")),
            P(("exp", "patch"), None),
            P(),
        ),
        out_specs=P("patch", None, "exp", None),
        check_vma=False,
    )
```

```python
import functools

import jax
import jax.numpy as jnp
from jax import lax
from jax.experimental import pallas as pl
from jax.experimental.pallas import tpu as pltpu
from jax.sharding import PartitionSpec as P

FILTERS = 6
TAPS = 21
BASIS = 16
CHUNKS = 4
CAP = 6
BF16 = jnp.bfloat16
F32 = jnp.float32


def trade_groups(vs):
    grp = lax.broadcasted_iota(jnp.int32, vs[0].shape, 1) // 16
    a = [v if i == 0 else pltpu.roll(v, 16 * i, 1) for i, v in enumerate(vs)]
    a = [a[-j % 8] for j in range(8)]
    for s in (1, 2, 4):
        pick = (grp & s) != 0
        a = [jnp.where(pick, a[(j - s) % 8], a[j]) for j in range(8)]
    return [v if j == 0 else pltpu.roll(v, 128 - 16 * j, 1) for j, v in enumerate(a)]


def trade_rows(a, b):
    upper = lax.broadcasted_iota(jnp.int32, a.shape, a.ndim - 2) < 4
    axis = a.ndim - 2
    return (
        jnp.where(upper, a, pltpu.roll(b, 4, axis)),
        jnp.where(upper, pltpu.roll(a, 4, axis), b),
    )


def strip_tiles(ref, tmp, by):
    rows = pl.ds(pl.multiple_of(by * 128, 128), 128)
    for b in range(4):
        tmp[b] = ref[0, rows, pl.ds(128 * b, 128)].astype(F32)
    result = []
    for b in range(4):
        halves = [
            trade_groups([tmp[b, pl.ds(8 * h + i, 8, stride=16), :] for i in range(8)])
            for h in range(2)
        ]
        result.append([jnp.concatenate([halves[0][j], halves[1][j]], axis=1) for j in range(8)])
    return result


def convolve(src, wts, acc, chunk, slot):
    lhs = [
        jnp.concatenate(
            [src[pl.ds(b * 8 + 2 * chunk + dx, 2)].reshape(64, 768) for b in range(4)], axis=0
        )
        for dx in range(3)
    ]
    total = jnp.dot(jnp.concatenate(lhs, axis=1), wts[...], preferred_element_type=F32)
    acc[slot] = total.reshape(4, 2, 32, 256)


def finish(var, tmp, acc, blocks, slot, chunks):
    def block_row(by, _):
        row0 = pl.multiple_of(by * 8, 8)
        for b, vs in enumerate(strip_tiles(var, tmp, by)):
            for i, c in enumerate(chunks):
                weight = 1.0 / jnp.concatenate(vs[2 * c : 2 * c + 2], axis=0)
                got = jnp.concatenate([acc[i, b, j, pl.ds(row0, 8), :] for j in range(2)], axis=0)
                blocks[slot, i, by * 4 + b, pl.ds(0, 16)] = (got * weight).astype(BF16)
                blocks[slot, i, by * 4 + b, pl.ds(16, 16)] = weight.astype(BF16)
        return 0

    lax.fori_loop(0, 4, block_row, 0)


def block_copy(blocks, outs, sems, i, b, where, slot):
    rows = pl.ds(pl.multiple_of(lax.rem(where, 8) * 32, 32), 32)
    return pltpu.make_async_copy(
        blocks.at[slot, i, b], outs[i].at[where // 8, rows], sems.at[slot]
    )


def drain(blocks, outs, sems, slot, count):
    def one(i, _):
        block_copy(blocks, outs, sems, 0, 0, 0, slot).wait()
        return 0

    lax.fori_loop(0, count, one, 0)


def scatter(dest, blocks, outs, sems, cell, cells, slot):
    def send(b, _):
        where = dest[cell * 16 + b]
        for i in range(len(outs)):
            block_copy(blocks, outs, sems, i, b, where, slot).start()
        return 0

    lax.fori_loop(0, 16, send, 0)

    @pl.when(cell == cells - 1)
    def _():
        real = cells * 16
        fill = outs[0].shape[0] * CAP - real

        def pad(k, _):
            where = dest[real + k]
            for i in range(len(outs)):
                block_copy(blocks, outs, sems, i, 0, where, slot).start()
            return 0

        lax.fori_loop(0, fill, pad, 0)
        drain(blocks, outs, sems, slot, (16 + fill) * len(outs))
        drain(blocks, outs, sems, 1 - slot, 16 * len(outs))


def build_weights(coef, bx, ry, rolled, wts):
    scaled = (coef[0] * ry[...]).astype(BF16)
    core = jnp.dot(bx[...], scaled, preferred_element_type=F32)
    side = jnp.zeros((48, 256), F32)
    wide = jnp.concatenate([side, core, side], axis=1)
    for r in range(8):
        turned = wide if r == 0 else pltpu.roll(wide, 1024 - 16 * r, 1)
        rolled[r] = turned.astype(BF16)
    for jy in range(48):
        start = 47 - jy
        r, base = start % 8, start // 8 * 128
        for dx in range(3):
            wts[pl.ds(dx * 768 + jy * 16, 16), :] = rolled[
                r, pl.ds(dx * 16, 16), pl.ds(base, 256)
            ]


def clear_edges(tiles, src):
    tiles[:, 0:8, :] = jnp.zeros((32, 8, 256), F32)
    tiles[:, 40:48, :] = jnp.zeros((32, 8, 256), F32)
    src[0] = jnp.zeros((32, 768), BF16)
    src[33] = jnp.zeros((32, 768), BF16)


def stack_rows(tiles, src, t):
    for dy in range(3):
        src[1 + t, :, pl.ds(dy * 256, 256)] = tiles[t, pl.ds(7 + dy, 32), :].astype(BF16)


def first_kernel(
    dest, img, var, coef, bx, ry, codes, out, tiled, *scratch
):
    tiles, src, tmp, rolled, wts, acc, blocks, sems, code_sem = scratch
    cell, cells = pl.program_id(0), pl.num_programs(0)
    slot = lax.rem(cell, 2)

    @pl.when(cell == 0)
    def _():
        clear_edges(tiles, src)

    build_weights(coef, bx, ry, rolled, wts)

    def tile_block(by, _):
        row0 = pl.multiple_of(8 + by * 8, 8)
        for b, vs in enumerate(strip_tiles(img, tmp, by)):
            for j, v in enumerate(vs):
                tiles[b * 8 + j, pl.ds(row0, 8), :] = v
        return 0

    lax.fori_loop(0, 4, tile_block, 0)

    def stack_some(b, _):
        for k in range(3):
            stack_rows(tiles, src, b * 8 + k)

        @pl.when(b > 0)
        def _():
            stack_rows(tiles, src, b * 8 - 1)

        return 0

    lax.fori_loop(0, 4, stack_some, 0)

    def keep(t, _):
        tiled[0, t] = tiles[t, pl.ds(8, 32), :].astype(BF16)
        return 0

    lax.fori_loop(0, 32, keep, 0, unroll=8)

    convolve(src, wts, acc, 0, 0)

    @pl.when(cell >= 2)
    def _():
        drain(blocks, [out], sems, slot, 16)

    finish(var, tmp, acc, blocks, slot, [0])
    scatter(dest, blocks, [out], sems, cell, cells, slot)

    @pl.when(cell == cells - 1)
    def _():
        copy = pltpu.make_async_copy(codes, out.at[:, pl.ds(CAP * 32, 16)], code_sem)
        copy.start()
        copy.wait()


def other_kernel(dest, tiled, var, coef, bx, ry, *rest):
    outs, rest = rest[: CHUNKS - 1], rest[CHUNKS - 1 :]
    tiles, src, tmp, rolled, wts, acc, blocks, sems = rest
    cell, cells = pl.program_id(0), pl.num_programs(0)
    slot = lax.rem(cell, 2)

    @pl.when(cell == 0)
    def _():
        clear_edges(tiles, src)

    build_weights(coef, bx, ry, rolled, wts)

    def stack_all(t, _):
        tiles[t, pl.ds(8, 32), :] = tiled[0, t].astype(F32)
        stack_rows(tiles, src, t)
        return 0

    lax.fori_loop(0, 32, stack_all, 0, unroll=4)

    for i in range(CHUNKS - 1):
        convolve(src, wts, acc, i + 1, i)

    @pl.when(cell >= 2)
    def _():
        drain(blocks, outs, sems, slot, 16 * len(outs))

    finish(var, tmp, acc, blocks, slot, list(range(1, CHUNKS)))
    scatter(dest, blocks, outs, sems, cell, cells, slot)


def match_cells(dest, images, variance, coef_rows, band_x, rows_y, codes):
    cells = images.shape[0]
    owners = codes.shape[0]
    out = jax.ShapeDtypeStruct((owners, CAP * 32, 256), BF16)
    out_codes = jax.ShapeDtypeStruct((owners, CAP * 32 + 16, 256), BF16)
    pixels = pl.BlockSpec((1, 512, 512), lambda i, d: (i, 0, 0))
    tiled_spec = pl.BlockSpec((1, 32, 32, 256), lambda i, d: (i, 0, 0, 0))
    tables = [
        pl.BlockSpec((1, 256, 1), lambda i, d: (i, 0, 0)),
        pl.BlockSpec((48, 256), lambda i, d: (0, 0)),
        pl.BlockSpec((256, 512), lambda i, d: (0, 0)),
    ]
    params = pltpu.CompilerParams(vmem_limit_bytes=48 * 2**20)
    cost = pl.CostEstimate(flops=9000000000, bytes_accessed=30000000, transcendentals=0)

    def scratch(chunks):
        return [
            pltpu.VMEM((32, 48, 256), F32),
            pltpu.VMEM((34, 32, 768), BF16),
            pltpu.VMEM((4, 128, 128), F32),
            pltpu.VMEM((8, 48, 1024), BF16),
            pltpu.VMEM((2304, 256), BF16),
            pltpu.VMEM((chunks, 4, 2, 32, 256), F32),
            pltpu.VMEM((2, chunks, 16, 32, 256), BF16),
            pltpu.SemaphoreType.DMA((2,)),
        ]

    first, tiled = pl.pallas_call(
        first_kernel,
        out_shape=[out_codes, jax.ShapeDtypeStruct((cells, 32, 32, 256), BF16)],
        grid_spec=pltpu.PrefetchScalarGridSpec(
            num_scalar_prefetch=1,
            grid=(cells,),
            in_specs=[
                pixels,
                pixels,
                *tables,
                pl.BlockSpec((owners, 16, 256), lambda i, d: (0, 0, 0)),
            ],
            out_specs=[pl.BlockSpec(memory_space=pl.ANY), tiled_spec],
            scratch_shapes=[*scratch(1), pltpu.SemaphoreType.DMA],
        ),
        compiler_params=params,
        cost_estimate=cost,
        name="match_first",
    )(dest, images, variance, coef_rows, band_x, rows_y, codes)
    others = pl.pallas_call(
        other_kernel,
        out_shape=[out] * (CHUNKS - 1),
        grid_spec=pltpu.PrefetchScalarGridSpec(
            num_scalar_prefetch=1,
            grid=(cells,),
            in_specs=[tiled_spec, pixels, *tables],
            out_specs=[pl.BlockSpec(memory_space=pl.ANY)] * (CHUNKS - 1),
            scratch_shapes=scratch(CHUNKS - 1),
        ),
        compiler_params=params,
        cost_estimate=cost,
        name="match_others",
    )(dest, tiled, variance, coef_rows, band_x, rows_y)
    return [first, *others]


def add_kernel(code, group, got, *rest):
    outs, acc = rest[:4], rest[4]
    step = pl.program_id(0)
    per = got.shape[0]

    @pl.when(step == 0)
    def _():
        acc[...] = jnp.zeros_like(acc)

    def one(i, _):
        for r in range(CAP):
            plane = code[(step * per + i) * CAP + r]
            acc[plane] += got[i, pl.ds(32 * r, 32), :].astype(F32)
        return 0

    lax.fori_loop(0, per, one, 0)

    @pl.when(step == pl.num_programs(0) - 1)
    def _():
        def put(p, _):
            for s, out in enumerate(outs):
                share = lax.rem(group[0] + s, 4)
                both = acc[share // 2 * 48 + p]
                fields = both.reshape(2, 16, 256)
                halves = trade_rows(fields[:, :8], fields[:, 8:])
                part = jnp.where(lax.rem(share, 2) == 0, halves[0], halves[1])
                out[p] = part.reshape(16, 256).astype(BF16)
            return 0

        lax.fori_loop(0, 48, put, 0)


def add_slots(code, group, got):
    steps = 4
    per = got.shape[0] // steps
    share = jax.ShapeDtypeStruct((48, 16, 256), BF16)
    return pl.pallas_call(
        add_kernel,
        out_shape=[share] * 4,
        grid_spec=pltpu.PrefetchScalarGridSpec(
            num_scalar_prefetch=2,
            grid=(steps,),
            in_specs=[pl.BlockSpec((per, got.shape[1], 256), lambda i, d, g: (i, 0, 0))],
            out_specs=[pl.BlockSpec((48, 16, 256), lambda i, d, g: (0, 0, 0))] * 4,
            scratch_shapes=[pltpu.VMEM((97, 32, 256), F32)],
        ),
        compiler_params=pltpu.CompilerParams(vmem_limit_bytes=48 * 2**20),
        cost_estimate=pl.CostEstimate(flops=6000000, bytes_accessed=6000000, transcendentals=0),
        name="add_slots",
    )(code, group, got)


def ratio_kernel(*refs):
    ins, out, lines = refs[:-2], refs[-2], refs[-1]

    def half(qx, _):
        def one(i, _):
            f = i * 2
            vs = []
            for c in range(CHUNKS):
                pair = []
                for k in range(2):
                    total = ins[4 * c][qx * 6 + f + k].astype(F32)
                    for s in range(1, 4):
                        total += ins[4 * c + s][qx * 6 + f + k].astype(F32)
                    pair.append(total[:8] / jnp.maximum(total[8:], 1.0))
                vs.extend(trade_rows(*pair))
            for h in range(2):
                got = trade_groups([v[:, 128 * h : 128 * h + 128] for v in vs])
                for k, line in enumerate(got):
                    lines[pl.ds(f * 64 + 8 * h + k, 8, stride=16), :] = line
            return 0

        lax.fori_loop(0, 3, one, 0)
        out[0, :, pl.ds(pl.multiple_of(qx * 128, 128), 128)] = lines[...]
        return 0

    lax.fori_loop(0, 2, half, 0)


def ratio(parts):
    patches = parts[0].shape[0] // 12
    out = pl.pallas_call(
        ratio_kernel,
        grid=(patches,),
        out_shape=jax.ShapeDtypeStruct((patches, FILTERS * 64, 256), F32),
        in_specs=[pl.BlockSpec((12, 16, 256), lambda i: (i, 0, 0))] * (4 * CHUNKS),
        out_specs=pl.BlockSpec((1, FILTERS * 64, 256), lambda i: (i, 0, 0)),
        scratch_shapes=[pltpu.VMEM((FILTERS * 64, 128), F32)],
        compiler_params=pltpu.CompilerParams(vmem_limit_bytes=48 * 2**20),
        name="ratio",
    )(*parts)
    return out.reshape(patches, FILTERS, 64, 256)


def tap_tables(kernel_x, kernel_y):
    jx = jnp.arange(48)[:, None]
    ix = jnp.arange(16)[None, :]
    pick = ((jx - ix - 6)[None] == jnp.arange(TAPS)[:, None, None]).astype(BF16)
    band_x = jnp.einsum("kt,tji->jki", kernel_x, pick, preferred_element_type=F32)
    band_x = band_x.astype(BF16).reshape(48, BASIS * 16)
    line = jnp.arange(512)
    tap = jnp.arange(TAPS)
    pick_y = (41 - (line // 16 + 16)[None, :] == tap[:, None]).astype(BF16)
    taps_y = jnp.dot(kernel_y, pick_y, preferred_element_type=F32).astype(BF16)
    row = jnp.arange(BASIS * 16)
    spread = (row[:, None] // 16 == jnp.arange(BASIS)[None, :]).astype(BF16)
    rows_y = jnp.dot(spread, taps_y, preferred_element_type=F32)
    rows_y = jnp.where(row[:, None] % 16 == line[None, :] % 16, rows_y, 0.0)
    return band_x, rows_y


def exchange(planes, groups):
    moved = [planes[0]]
    for s in range(1, groups):
        ring = [(i, (i + s) % groups) for i in range(groups)]
        moved.append(lax.ppermute(planes[s], "exp", ring))
    return moved


def on_device(images, variance, kernel_x, kernel_y, coef, exposure_filter, block_patch, patch_home):
    cell_count = images.shape[0]
    owner_count = lax.axis_size("patch")
    patches_local = patch_home.shape[0] // owner_count
    block_count = cell_count * 16
    slots = owner_count * CAP

    targets = block_patch.reshape(-1)
    patch_index = targets // 4
    quadrant = targets % 4
    home_slot = jnp.sum(
        jnp.where(
            patch_index[:, None] == jnp.arange(patch_home.shape[0])[None, :], patch_home[None, :], 0
        ),
        axis=1,
    )
    owner_index = home_slot // patches_local
    local_patch = home_slot % patches_local
    band_index = jnp.repeat(exposure_filter, 16)
    order = jnp.arange(block_count)
    earlier = order[None, :] < order[:, None]
    rank = jnp.sum((owner_index[:, None] == owner_index[None, :]) & earlier, axis=1)
    dest = owner_index * CAP + rank
    slot_ids = jnp.arange(slots)
    hits = dest[None, :] == slot_ids[:, None]
    code = (
        (quadrant // 2) * 48 + (local_patch * 2 + quadrant % 2) * FILTERS + band_index
    )
    slot_code = jnp.min(jnp.where(hits, code[None, :], 96), axis=1)
    empty = slot_code == 96
    empty_rank = jnp.sum(empty[None, :] & (slot_ids[None, :] < slot_ids[:, None]), axis=1)
    place = jnp.arange(slots - block_count)
    spare = jnp.sum(
        jnp.where(
            empty[None, :] & (empty_rank[None, :] == place[:, None]), slot_ids[None, :], 0
        ),
        axis=1,
    )
    dest_all = jnp.concatenate([dest, spare]).astype(jnp.int32)
    dest_all = dest_all // CAP * 8 + dest_all % CAP
    codes = jnp.pad(
        slot_code.astype(BF16).reshape(owner_count, 1, CAP), ((0, 0), (0, 15), (0, 256 - CAP))
    )
    band_x, rows_y = tap_tables(kernel_x, kernel_y)
    coef_rows = jnp.repeat(coef, 16, axis=1)[:, :, None]
    sent = match_cells(dest_all, images, variance, coef_rows, band_x, rows_y, codes)

    groups = lax.axis_size("exp")
    group = lax.axis_index("exp").reshape(1)
    def send(part):
        return lax.all_to_all(part, "patch", 0, 0, tiled=True)

    def add(got):
        return add_slots(got_code, group, got)

    hold = lax.optimization_barrier
    got_0 = send(sent[0])
    got_code = got_0[:, CAP * 32, :CAP].reshape(-1).astype(jnp.int32)
    planes_0 = add(got_0)
    planes_1 = add(send(sent[1]))
    part_2, planes_0 = hold((sent[2], planes_0))
    share_0 = exchange(planes_0, groups)
    planes_2 = add(send(part_2))
    part_3, planes_1, share_0 = hold((sent[3], planes_1, share_0))
    share_1 = exchange(planes_1, groups)
    got_3 = send(part_3)
    share_2 = exchange(planes_2, groups)
    got_3, share_1, share_2 = hold((got_3, share_1, share_2))
    share_3 = exchange(add(got_3), groups)
    return ratio([*share_0, *share_1, *share_2, *share_3])


def solution(mesh):
    return jax.shard_map(
        on_device,
        mesh=mesh,
        in_specs=(
            P(("exp", "patch"), None, None),
            P(("exp", "patch"), None, None),
            P(),
            P(),
            P(("exp", "patch"), None),
            P(("exp", "patch")),
            P(("exp", "patch"), None),
            P(),
        ),
        out_specs=P("patch", None, "exp", None),
        check_vma=False,
    )
```

```python
import functools

import jax
import jax.numpy as jnp
from jax import lax
from jax.experimental import pallas as pl
from jax.experimental.pallas import tpu as pltpu
from jax.sharding import PartitionSpec as P

FILTERS = 6
TAPS = 21
BASIS = 16
CHUNKS = 4
CAP = 4
EXTRA = 2
ALL = CAP + EXTRA
LOOSE = 2
NONE = 96
BF16 = jnp.bfloat16
F32 = jnp.float32


def trade_groups(vs):
    grp = lax.broadcasted_iota(jnp.int32, vs[0].shape, 1) // 16
    a = [v if i == 0 else pltpu.roll(v, 16 * i, 1) for i, v in enumerate(vs)]
    a = [a[-j % 8] for j in range(8)]
    for s in (1, 2, 4):
        pick = (grp & s) != 0
        a = [jnp.where(pick, a[(j - s) % 8], a[j]) for j in range(8)]
    return [v if j == 0 else pltpu.roll(v, 128 - 16 * j, 1) for j, v in enumerate(a)]


def trade_rows(a, b):
    upper = lax.broadcasted_iota(jnp.int32, a.shape, a.ndim - 2) < 4
    axis = a.ndim - 2
    return (
        jnp.where(upper, a, pltpu.roll(b, 4, axis)),
        jnp.where(upper, pltpu.roll(a, 4, axis), b),
    )


def block_tiles(tmp, b):
    halves = [
        trade_groups([tmp[b, pl.ds(8 * h + i, 8, stride=16), :] for i in range(8)])
        for h in range(2)
    ]
    return [jnp.concatenate([halves[0][j], halves[1][j]], axis=1) for j in range(8)]


def strip_tiles(ref, tmp, by):
    rows = pl.ds(pl.multiple_of(by * 128, 128), 128)
    for b in range(4):
        tmp[b] = ref[0, rows, pl.ds(128 * b, 128)].astype(F32)
    return [block_tiles(tmp, b) for b in range(4)]


def convolve(src, wts, acc, chunk, slot):
    lhs = [
        jnp.concatenate(
            [src[pl.ds(b * 8 + 2 * chunk + dx, 2)].reshape(64, 768) for b in range(4)], axis=0
        )
        for dx in range(3)
    ]
    total = jnp.dot(jnp.concatenate(lhs, axis=1), wts[...], preferred_element_type=F32)
    acc[slot] = total.reshape(4, 2, 32, 256)


def finish(var, tmp, acc, blocks, slot, chunks):
    def block_row(by, _):
        row0 = pl.multiple_of(by * 8, 8)
        for b, vs in enumerate(strip_tiles(var, tmp, by)):
            for i, c in enumerate(chunks):
                weight = 1.0 / jnp.concatenate(vs[2 * c : 2 * c + 2], axis=0)
                got = jnp.concatenate([acc[i, b, j, pl.ds(row0, 8), :] for j in range(2)], axis=0)
                blocks[slot, i, by * 4 + b, pl.ds(0, 16)] = (got * weight).astype(BF16)
                blocks[slot, i, by * 4 + b, pl.ds(16, 16)] = weight.astype(BF16)
        return 0

    lax.fori_loop(0, 4, block_row, 0)


def drain(blocks, outs, sems, slot):
    def one(i, _):
        pltpu.make_async_copy(blocks.at[slot, 0, 0], outs[0][0].at[0, pl.ds(0, 32)], sems.at[slot]).wait()
        return 0

    lax.fori_loop(0, 16 * len(outs), one, 0)


def scatter(dest, blocks, outs, sems, cell, cells, slot):
    def send(b, _):
        where = dest[cell * 16 + b]
        owner, rank = where // 8, lax.rem(where, 8)

        def copy(i, target):
            pltpu.make_async_copy(blocks.at[slot, i, b], target, sems.at[slot]).start()

        def rows(k):
            return pl.ds(pl.multiple_of(k * 32, 32), 32)

        if outs[0][1] is None:
            for i, (main, _) in enumerate(outs):
                copy(i, main.at[owner, rows(rank)])
            return 0

        @pl.when(rank < CAP)
        def _():
            for i, (main, _) in enumerate(outs):
                copy(i, main.at[owner, rows(rank)])

        @pl.when(rank >= CAP)
        def _():
            for i, (_, extra) in enumerate(outs):
                copy(i, extra.at[owner, rows(rank - CAP)])

        return 0

    lax.fori_loop(0, 16, send, 0)

    @pl.when(cell == cells - 1)
    def _():
        drain(blocks, outs, sems, slot)
        drain(blocks, outs, sems, 1 - slot)


def build_weights(coef, bx, ry, rolled, wts):
    scaled = (coef[0] * ry[...]).astype(BF16)
    core = jnp.dot(bx[...], scaled, preferred_element_type=F32)
    side = jnp.zeros((48, 256), F32)
    wide = jnp.concatenate([side, core, side], axis=1)
    for r in range(8):
        turned = wide if r == 0 else pltpu.roll(wide, 1024 - 16 * r, 1)
        rolled[r] = turned.astype(BF16)
    for jy in range(48):
        start = 47 - jy
        r, base = start % 8, start // 8 * 128
        for dx in range(3):
            wts[pl.ds(dx * 768 + jy * 16, 16), :] = rolled[
                r, pl.ds(dx * 16, 16), pl.ds(base, 256)
            ]


def clear_edges(tiles, src):
    tiles[:, 0:8, :] = jnp.zeros((32, 8, 256), F32)
    tiles[:, 40:48, :] = jnp.zeros((32, 8, 256), F32)
    src[0] = jnp.zeros((32, 768), BF16)
    src[33] = jnp.zeros((32, 768), BF16)


def stack_rows(tiles, src, t):
    for dy in range(3):
        src[1 + t, :, pl.ds(dy * 256, 256)] = tiles[t, pl.ds(7 + dy, 32), :].astype(BF16)


def first_kernel(
    dest, img, var, coef, bx, ry, codes, out, tiled, free, *scratch
):
    tiles, src, tmp, rolled, wts, acc, blocks, sems, code_sem, wide = scratch
    cell, cells = pl.program_id(0), pl.num_programs(0)
    slot = lax.rem(cell, 2)

    @pl.when(cell == 0)
    def _():
        clear_edges(tiles, src)

    build_weights(coef, bx, ry, rolled, wts)

    def tile_block(by, _):
        row0 = pl.multiple_of(8 + by * 8, 8)
        for b, vs in enumerate(strip_tiles(img, tmp, by)):
            for j, v in enumerate(vs):
                tiles[b * 8 + j, pl.ds(row0, 8), :] = v
        return 0

    lax.fori_loop(0, 4, tile_block, 0)

    def stack_some(b, _):
        for k in range(3):
            stack_rows(tiles, src, b * 8 + k)

        @pl.when(b > 0)
        def _():
            stack_rows(tiles, src, b * 8 - 1)

        return 0

    lax.fori_loop(0, 4, stack_some, 0)

    def keep(t, _):
        tiled[0, t] = tiles[t, pl.ds(8, 32), :].astype(BF16)
        return 0

    lax.fori_loop(0, 32, keep, 0, unroll=8)

    convolve(src, wts, acc, 0, 0)

    @pl.when(cell >= 2)
    def _():
        drain(blocks, [(out, None)], sems, slot)

    finish(var, tmp, acc, blocks, slot, [0])
    scatter(dest, blocks, [(out, None)], sems, cell, cells, slot)

    for k in range(LOOSE):
        which = dest[cells * 16 + k]

        @pl.when(which // 16 == cell)
        def _(k=k, which=which):
            by, b = lax.rem(which, 16) // 4, lax.rem(which, 4)
            for j in range(3, 8):
                stack_rows(tiles, src, b * 8 + j)
            lhs = [src[pl.ds(b * 8 + dx, 8)].reshape(256, 768) for dx in range(3)]
            total = jnp.dot(
                jnp.concatenate(lhs, axis=1), wts[...], preferred_element_type=F32
            )
            wide[...] = total.reshape(8, 32, 256)
            rows = pl.ds(pl.multiple_of(by * 128, 128), 128)
            cols = pl.ds(pl.multiple_of(b * 128, 128), 128)
            tmp[0] = var[0, rows, cols].astype(F32)
            vs = block_tiles(tmp, 0)
            row0 = pl.multiple_of(by * 8, 8)
            for c in range(1, CHUNKS):
                weight = 1.0 / jnp.concatenate(vs[2 * c : 2 * c + 2], axis=0)
                got = jnp.concatenate(
                    [wide[2 * c + j, pl.ds(row0, 8), :] for j in range(2)], axis=0
                )
                free[c - 1, k, pl.ds(0, 16)] = (got * weight).astype(BF16)
                free[c - 1, k, pl.ds(16, 16)] = weight.astype(BF16)

    @pl.when(cell == cells - 1)
    def _():
        copy = pltpu.make_async_copy(codes, out.at[:, pl.ds(ALL * 32, 16)], code_sem)
        copy.start()
        copy.wait()


def other_kernel(dest, tiled, var, coef, bx, ry, *rest):
    outs, rest = rest[: 2 * (CHUNKS - 1)], rest[2 * (CHUNKS - 1) :]
    outs = [outs[2 * i : 2 * i + 2] for i in range(CHUNKS - 1)]
    tiles, src, tmp, rolled, wts, acc, blocks, sems = rest
    cell, cells = pl.program_id(0), pl.num_programs(0)
    slot = lax.rem(cell, 2)

    @pl.when(cell == 0)
    def _():
        clear_edges(tiles, src)

    build_weights(coef, bx, ry, rolled, wts)

    def stack_all(t, _):
        tiles[t, pl.ds(8, 32), :] = tiled[0, t].astype(F32)
        stack_rows(tiles, src, t)
        return 0

    lax.fori_loop(0, 32, stack_all, 0, unroll=4)

    for i in range(CHUNKS - 1):
        convolve(src, wts, acc, i + 1, i)

    @pl.when(cell >= 2)
    def _():
        drain(blocks, outs, sems, slot)

    finish(var, tmp, acc, blocks, slot, list(range(1, CHUNKS)))
    scatter(dest, blocks, outs, sems, cell, cells, slot)


def match_cells(dest, images, variance, coef_rows, band_x, rows_y, codes):
    cells = images.shape[0]
    owners = codes.shape[0]
    out = [
        jax.ShapeDtypeStruct((owners, CAP * 32, 256), BF16),
        jax.ShapeDtypeStruct((owners, EXTRA * 32, 256), BF16),
    ]
    out_codes = jax.ShapeDtypeStruct((owners, ALL * 32 + 16, 256), BF16)
    pixels = pl.BlockSpec((1, 512, 512), lambda i, d: (i, 0, 0))
    tiled_spec = pl.BlockSpec((1, 32, 32, 256), lambda i, d: (i, 0, 0, 0))
    tables = [
        pl.BlockSpec((1, 256, 1), lambda i, d: (i, 0, 0)),
        pl.BlockSpec((48, 256), lambda i, d: (0, 0)),
        pl.BlockSpec((256, 512), lambda i, d: (0, 0)),
    ]
    params = pltpu.CompilerParams(vmem_limit_bytes=48 * 2**20)
    cost = pl.CostEstimate(flops=9000000000, bytes_accessed=30000000, transcendentals=0)

    def scratch(chunks):
        return [
            pltpu.VMEM((32, 48, 256), F32),
            pltpu.VMEM((34, 32, 768), BF16),
            pltpu.VMEM((4, 128, 128), F32),
            pltpu.VMEM((8, 48, 1024), BF16),
            pltpu.VMEM((2304, 256), BF16),
            pltpu.VMEM((chunks, 4, 2, 32, 256), F32),
            pltpu.VMEM((2, chunks, 16, 32, 256), BF16),
            pltpu.SemaphoreType.DMA((2,)),
        ]

    first, tiled, free = pl.pallas_call(
        first_kernel,
        out_shape=[
            out_codes,
            jax.ShapeDtypeStruct((cells, 32, 32, 256), BF16),
            jax.ShapeDtypeStruct((CHUNKS - 1, LOOSE, 32, 256), BF16),
        ],
        grid_spec=pltpu.PrefetchScalarGridSpec(
            num_scalar_prefetch=1,
            grid=(cells,),
            in_specs=[
                pixels,
                pixels,
                *tables,
                pl.BlockSpec((owners, 16, 256), lambda i, d: (0, 0, 0)),
            ],
            out_specs=[
                pl.BlockSpec(memory_space=pl.ANY),
                tiled_spec,
                pl.BlockSpec((CHUNKS - 1, LOOSE, 32, 256), lambda i, d: (0, 0, 0, 0)),
            ],
            scratch_shapes=[
                *scratch(1),
                pltpu.SemaphoreType.DMA,
                pltpu.VMEM((8, 32, 256), F32),
            ],
        ),
        compiler_params=params,
        cost_estimate=cost,
        name="match_first",
    )(dest, images, variance, coef_rows, band_x, rows_y, codes)
    others = pl.pallas_call(
        other_kernel,
        out_shape=out * (CHUNKS - 1),
        grid_spec=pltpu.PrefetchScalarGridSpec(
            num_scalar_prefetch=1,
            grid=(cells,),
            in_specs=[tiled_spec, pixels, *tables],
            out_specs=[pl.BlockSpec(memory_space=pl.ANY)] * (2 * (CHUNKS - 1)),
            scratch_shapes=scratch(CHUNKS - 1),
        ),
        compiler_params=params,
        cost_estimate=cost,
        name="match_others",
    )(dest, tiled, variance, coef_rows, band_x, rows_y)
    return free, [first, *others[0::2]], others[1::2]


def add_kernel(begin, code, group, got, *rest):
    free, outs, acc = rest[:-5], rest[-5:-1], rest[-1]
    step = pl.program_id(0)
    per = got.shape[0]

    @pl.when(step == 0)
    def _():
        acc[...] = jnp.zeros_like(acc)

    def one(i, _):
        at = (step * per + i) * 8
        for r in range(got.shape[1] // 32):
            acc[code[at + begin + r]] += got[i, pl.ds(32 * r, 32), :].astype(F32)
        for r in range(LOOSE if free else 0):
            plane = code[at + ALL + r]

            @pl.when(plane != NONE)
            def _(r=r, plane=plane):
                acc[plane] += free[0][i, pl.ds(32 * r, 32), :].astype(F32)

        return 0

    lax.fori_loop(0, per, one, 0)

    @pl.when(step == pl.num_programs(0) - 1)
    def _():
        def put(p, _):
            for s, out in enumerate(outs):
                share = lax.rem(group[0] + s, 4)
                both = acc[share // 2 * 48 + p]
                fields = both.reshape(2, 16, 256)
                halves = trade_rows(fields[:, :8], fields[:, 8:])
                part = jnp.where(lax.rem(share, 2) == 0, halves[0], halves[1])
                out[p] = part.reshape(16, 256).astype(BF16)
            return 0

        lax.fori_loop(0, 48, put, 0, unroll=2)
        for out in outs:
            out[48] = jnp.full((16, 256), group[1].astype(F32), F32).astype(BF16)


def add_slots(code, group, got, begin, free=None, part=0):
    steps = 4
    per = got.shape[0] // steps
    count = got.shape[1] // 32 * 32
    share = jax.ShapeDtypeStruct((49, 16, 256), BF16)
    specs = [pl.BlockSpec((per, count, 256), lambda i, d, g: (i, 0, 0))]
    if free is not None:
        specs.append(pl.BlockSpec((per, LOOSE * 32, 256), lambda i, d, g: (i, part, 0)))
    return pl.pallas_call(
        functools.partial(add_kernel, begin),
        out_shape=[share] * 4,
        grid_spec=pltpu.PrefetchScalarGridSpec(
            num_scalar_prefetch=2,
            grid=(steps,),
            in_specs=specs,
            out_specs=[pl.BlockSpec((49, 16, 256), lambda i, d, g: (0, 0, 0))] * 4,
            scratch_shapes=[pltpu.VMEM((NONE + 1, 32, 256), F32)],
        ),
        compiler_params=pltpu.CompilerParams(vmem_limit_bytes=48 * 2**20),
        cost_estimate=pl.CostEstimate(flops=6000000, bytes_accessed=6000000, transcendentals=0),
        name="add_slots",
    )(code, group, got, *([] if free is None else [free]))


def ratio_kernel(counts, *refs):
    ins, out, lines = refs[:-2], refs[-2], refs[-1]
    starts = [sum(counts[:c]) for c in range(CHUNKS)]

    def half(qx, _):
        def one(i, _):
            f = i * 2
            vs = []
            for c in range(CHUNKS):
                pair = []
                for k in range(2):
                    total = ins[starts[c]][qx * 6 + f + k].astype(F32)
                    for s in range(1, counts[c]):
                        total += ins[starts[c] + s][qx * 6 + f + k].astype(F32)
                    pair.append(total[:8] / jnp.maximum(total[8:], 1.0))
                vs.extend(trade_rows(*pair))
            for h in range(2):
                got = trade_groups([v[:, 128 * h : 128 * h + 128] for v in vs])
                for k, line in enumerate(got):
                    lines[pl.ds(f * 64 + 8 * h + k, 8, stride=16), :] = line
            return 0

        lax.fori_loop(0, 3, one, 0)
        out[0, :, pl.ds(pl.multiple_of(qx * 128, 128), 128)] = lines[...]
        return 0

    lax.fori_loop(0, 2, half, 0)


def ratio(shares):
    counts = [len(share) for share in shares]
    parts = [x for share in shares for x in share]
    patches = parts[0].shape[0] // 12
    out = pl.pallas_call(
        functools.partial(ratio_kernel, counts),
        grid=(patches,),
        out_shape=jax.ShapeDtypeStruct((patches, FILTERS * 64, 256), F32),
        in_specs=[pl.BlockSpec((12, 16, 256), lambda i: (i, 0, 0))] * len(parts),
        out_specs=pl.BlockSpec((1, FILTERS * 64, 256), lambda i: (i, 0, 0)),
        scratch_shapes=[pltpu.VMEM((FILTERS * 64, 128), F32)],
        compiler_params=pltpu.CompilerParams(vmem_limit_bytes=48 * 2**20),
        name="ratio",
    )(*parts)
    return out.reshape(patches, FILTERS, 64, 256)


def tap_tables(kernel_x, kernel_y):
    jx = jnp.arange(48)[:, None]
    ix = jnp.arange(16)[None, :]
    pick = ((jx - ix - 6)[None] == jnp.arange(TAPS)[:, None, None]).astype(BF16)
    band_x = jnp.einsum("kt,tji->jki", kernel_x, pick, preferred_element_type=F32)
    band_x = band_x.astype(BF16).reshape(48, BASIS * 16)
    line = jnp.arange(512)
    tap = jnp.arange(TAPS)
    pick_y = (41 - (line // 16 + 16)[None, :] == tap[:, None]).astype(BF16)
    taps_y = jnp.dot(kernel_y, pick_y, preferred_element_type=F32).astype(BF16)
    row = jnp.arange(BASIS * 16)
    spread = (row[:, None] // 16 == jnp.arange(BASIS)[None, :]).astype(BF16)
    rows_y = jnp.dot(spread, taps_y, preferred_element_type=F32)
    rows_y = jnp.where(row[:, None] % 16 == line[None, :] % 16, rows_y, 0.0)
    return band_x, rows_y


def exchange(planes, groups):
    moved = [planes[0]]
    for s in range(1, groups):
        ring = [(i, (i + s) % groups) for i in range(groups)]
        moved.append(lax.ppermute(planes[s], "exp", ring))
    return moved


def on_device(images, variance, kernel_x, kernel_y, coef, exposure_filter, block_patch, patch_home):
    cell_count = images.shape[0]
    owner_count = lax.axis_size("patch")
    patches_local = patch_home.shape[0] // owner_count
    block_count = cell_count * 16

    targets = block_patch.reshape(-1)
    patch_index = targets // 4
    quadrant = targets % 4
    home_slot = jnp.sum(
        jnp.where(
            patch_index[:, None] == jnp.arange(patch_home.shape[0])[None, :], patch_home[None, :], 0
        ),
        axis=1,
    )
    owner_index = home_slot // patches_local
    local_patch = home_slot % patches_local
    band_index = jnp.repeat(exposure_filter, 16)
    order = jnp.arange(block_count)
    earlier = order[None, :] < order[:, None]
    rank = jnp.sum((owner_index[:, None] == owner_index[None, :]) & earlier, axis=1)
    late = rank >= CAP
    late_rank = jnp.sum(late[None, :] & earlier, axis=1)
    loose = late & (late_rank < LOOSE)
    more = jnp.any(late & (late_rank >= LOOSE))
    which = loose & (late_rank == jnp.arange(LOOSE)[:, None])
    which = jnp.max(jnp.where(which, order, -16), axis=1)
    dest = jnp.concatenate([owner_index * 8 + rank, which]).astype(jnp.int32)
    code = (
        (quadrant // 2) * 48 + (local_patch * 2 + quadrant % 2) * FILTERS + band_index
    )
    place = jnp.where(loose, ALL + late_rank, -1)
    more_place = jnp.where(late & ~loose, rank, -1)
    owners = jnp.arange(owner_count)[:, None, None]
    row = jnp.arange(16)[:, None]
    here = (rank == row) | (place == row) | (more_place + 5 == row) & (row >= 9)
    codes = jnp.min(jnp.where((owner_index == owners) & here, code, NONE), axis=2)
    codes = jnp.where(jnp.arange(16) == 8, more.astype(code.dtype), codes)
    codes = jnp.pad(codes.astype(BF16)[:, None, :], ((0, 0), (0, 15), (0, 240)))

    band_x, rows_y = tap_tables(kernel_x, kernel_y)
    coef_rows = jnp.repeat(coef, 16, axis=1)[:, :, None]
    free, mains, extras = match_cells(dest, images, variance, coef_rows, band_x, rows_y, codes)

    groups = lax.axis_size("exp")
    def send(part):
        return lax.all_to_all(part, "patch", 0, 0, tiled=True)

    gathered = lax.all_gather(free.reshape(-1, 256), "patch")
    got_0 = send(mains[0])
    head = got_0[:, ALL * 32, :16].astype(jnp.int32)
    got_code = head[:, :8].reshape(-1)
    group = jnp.stack([lax.axis_index("exp"), jnp.max(head[:, 8])])

    def add(got, c):
        return add_slots(got_code, group, got, 0, gathered, c - 1)

    hold = lax.optimization_barrier
    planes_0 = add_slots(got_code, group, got_0, 0)
    share_0 = exchange(planes_0, groups)
    got_1 = send(mains[1])
    part_2, own = hold((mains[2], planes_0[0]))
    share_0[0] = own
    planes_1 = add(got_1, 1)
    share_1 = exchange(planes_1, groups)
    got_2 = send(part_2)
    part_3, share_0, share_1[0] = hold((mains[3], share_0, share_1[0]))
    share_2 = exchange(add(got_2, 2), groups)
    got_3, share_1 = hold((send(part_3), share_1))
    share_3 = exchange(add(got_3, 3), groups)
    shares = [share_0, share_1, share_2, share_3]

    def plain(shares, extras, head):
        return ratio(shares)

    def with_more(shares, extras, head):
        codes = jnp.concatenate([head[:, :CAP], head[:, 9 : 9 + EXTRA], head[:, :2]], axis=1)
        parts = [shares[0]]
        for share, extra in zip(shares[1:], extras, strict=True):
            planes = add_slots(codes.reshape(-1), group, send(extra), CAP)
            parts.append([*share, *exchange(planes, groups)])
        return ratio(parts)

    more = functools.reduce(jnp.maximum, [x[48, 0, 0] for x in share_0]) > 0
    return lax.cond(more, with_more, plain, shares, extras, head)


def solution(mesh):
    return jax.shard_map(
        on_device,
        mesh=mesh,
        in_specs=(
            P(("exp", "patch"), None, None),
            P(("exp", "patch"), None, None),
            P(),
            P(),
            P(("exp", "patch"), None),
            P(("exp", "patch")),
            P(("exp", "patch"), None),
            P(),
        ),
        out_specs=P("patch", None, "exp", None),
        check_vma=False,
    )
```

```python
import functools

import jax
import jax.numpy as jnp
from jax import lax
from jax.experimental import pallas as pl
from jax.experimental.pallas import tpu as pltpu
from jax.sharding import PartitionSpec as P

FILTERS = 6
TAPS = 21
BASIS = 16
CHUNKS = 4
CAP = 4
EXTRA = 2
ALL = CAP + EXTRA
LOOSE = 2
NONE = 96
BF16 = jnp.bfloat16
F32 = jnp.float32


def trade_groups(vs):
    grp = lax.broadcasted_iota(jnp.int32, vs[0].shape, 1) // 16
    a = [v if i == 0 else pltpu.roll(v, 16 * i, 1) for i, v in enumerate(vs)]
    a = [a[-j % 8] for j in range(8)]
    for s in (1, 2, 4):
        pick = (grp & s) != 0
        a = [jnp.where(pick, a[(j - s) % 8], a[j]) for j in range(8)]
    return [v if j == 0 else pltpu.roll(v, 128 - 16 * j, 1) for j, v in enumerate(a)]


def trade_rows(a, b):
    upper = lax.broadcasted_iota(jnp.int32, a.shape, a.ndim - 2) < 4
    axis = a.ndim - 2
    return (
        jnp.where(upper, a, pltpu.roll(b, 4, axis)),
        jnp.where(upper, pltpu.roll(a, 4, axis), b),
    )


def block_tiles(tmp, b):
    halves = [
        trade_groups([tmp[b, pl.ds(8 * h + i, 8, stride=16), :] for i in range(8)])
        for h in range(2)
    ]
    return [jnp.concatenate([halves[0][j], halves[1][j]], axis=1) for j in range(8)]


def strip_tiles(ref, tmp, by):
    rows = pl.ds(pl.multiple_of(by * 128, 128), 128)
    for b in range(4):
        tmp[b] = ref[0, rows, pl.ds(128 * b, 128)].astype(F32)
    return [block_tiles(tmp, b) for b in range(4)]


def convolve(src, wts, acc, chunk, slot):
    lhs = [
        jnp.concatenate(
            [src[pl.ds(b * 8 + 2 * chunk + dx, 2)].reshape(64, 768) for b in range(4)], axis=0
        )
        for dx in range(3)
    ]
    total = jnp.dot(jnp.concatenate(lhs, axis=1), wts[...], preferred_element_type=F32)
    acc[slot] = total.reshape(4, 2, 32, 256)


def finish(var, tmp, acc, blocks, slot, chunks):
    def block_row(by, _):
        row0 = pl.multiple_of(by * 8, 8)
        for b, vs in enumerate(strip_tiles(var, tmp, by)):
            for i, c in enumerate(chunks):
                weight = 1.0 / jnp.concatenate(vs[2 * c : 2 * c + 2], axis=0)
                got = jnp.concatenate([acc[i, b, j, pl.ds(row0, 8), :] for j in range(2)], axis=0)
                blocks[slot, i, by * 4 + b, pl.ds(0, 16)] = (got * weight).astype(BF16)
                blocks[slot, i, by * 4 + b, pl.ds(16, 16)] = weight.astype(BF16)
        return 0

    lax.fori_loop(0, 4, block_row, 0)


def drain(blocks, outs, sems, slot):
    def one(i, _):
        pltpu.make_async_copy(blocks.at[slot, 0, 0], outs[0][0].at[0, pl.ds(0, 32)], sems.at[slot]).wait()
        return 0

    lax.fori_loop(0, 16 * len(outs), one, 0)


def scatter(dest, blocks, outs, sems, cell, cells, slot):
    def send(b, _):
        where = dest[cell * 16 + b]
        owner, rank = where // 8, lax.rem(where, 8)

        def copy(i, target):
            pltpu.make_async_copy(blocks.at[slot, i, b], target, sems.at[slot]).start()

        def rows(k):
            return pl.ds(pl.multiple_of(k * 32, 32), 32)

        if outs[0][1] is None:
            for i, (main, _) in enumerate(outs):
                copy(i, main.at[owner, rows(rank)])
            return 0

        @pl.when(rank < CAP)
        def _():
            for i, (main, _) in enumerate(outs):
                copy(i, main.at[owner, rows(rank)])

        @pl.when(rank >= CAP)
        def _():
            for i, (_, extra) in enumerate(outs):
                copy(i, extra.at[owner, rows(rank - CAP)])

        return 0

    lax.fori_loop(0, 16, send, 0)

    @pl.when(cell == cells - 1)
    def _():
        drain(blocks, outs, sems, slot)
        drain(blocks, outs, sems, 1 - slot)


def build_weights(coef, bx, ry, rolled, wts):
    scaled = (coef[0] * ry[...]).astype(BF16)
    core = jnp.dot(bx[...], scaled, preferred_element_type=F32)
    side = jnp.zeros((48, 256), F32)
    wide = jnp.concatenate([side, core, side], axis=1)
    for r in range(8):
        turned = wide if r == 0 else pltpu.roll(wide, 1024 - 16 * r, 1)
        rolled[r] = turned.astype(BF16)
    for jy in range(48):
        start = 47 - jy
        r, base = start % 8, start // 8 * 128
        for dx in range(3):
            wts[pl.ds(dx * 768 + jy * 16, 16), :] = rolled[
                r, pl.ds(dx * 16, 16), pl.ds(base, 256)
            ]


def clear_edges(tiles, src):
    tiles[:, 0:8, :] = jnp.zeros((32, 8, 256), F32)
    tiles[:, 40:48, :] = jnp.zeros((32, 8, 256), F32)
    src[0] = jnp.zeros((32, 768), BF16)
    src[33] = jnp.zeros((32, 768), BF16)


def stack_rows(tiles, src, t):
    for dy in range(3):
        src[1 + t, :, pl.ds(dy * 256, 256)] = tiles[t, pl.ds(7 + dy, 32), :].astype(BF16)


def first_kernel(
    dest, img, var, coef, bx, ry, codes, out, tiled, free, *scratch
):
    tiles, src, tmp, rolled, wts, acc, blocks, sems, code_sem, wide = scratch
    cell, cells = pl.program_id(0), pl.num_programs(0)
    slot = lax.rem(cell, 2)

    @pl.when(cell == 0)
    def _():
        clear_edges(tiles, src)

    build_weights(coef, bx, ry, rolled, wts)

    def tile_block(by, _):
        row0 = pl.multiple_of(8 + by * 8, 8)
        for b, vs in enumerate(strip_tiles(img, tmp, by)):
            for j, v in enumerate(vs):
                tiles[b * 8 + j, pl.ds(row0, 8), :] = v
        return 0

    lax.fori_loop(0, 4, tile_block, 0)

    def stack_some(b, _):
        for k in range(3):
            stack_rows(tiles, src, b * 8 + k)

        @pl.when(b > 0)
        def _():
            stack_rows(tiles, src, b * 8 - 1)

        return 0

    lax.fori_loop(0, 4, stack_some, 0)

    def keep(t, _):
        tiled[0, t] = tiles[t, pl.ds(8, 32), :].astype(BF16)
        return 0

    lax.fori_loop(0, 32, keep, 0, unroll=8)

    convolve(src, wts, acc, 0, 0)

    @pl.when(cell >= 2)
    def _():
        drain(blocks, [(out, None)], sems, slot)

    finish(var, tmp, acc, blocks, slot, [0])
    scatter(dest, blocks, [(out, None)], sems, cell, cells, slot)

    for k in range(LOOSE):
        which = dest[cells * 16 + k]

        @pl.when(which // 16 == cell)
        def _(k=k, which=which):
            by, b = lax.rem(which, 16) // 4, lax.rem(which, 4)
            for j in range(3, 8):
                stack_rows(tiles, src, b * 8 + j)
            lhs = [src[pl.ds(b * 8 + dx, 8)].reshape(256, 768) for dx in range(3)]
            total = jnp.dot(
                jnp.concatenate(lhs, axis=1), wts[...], preferred_element_type=F32
            )
            wide[...] = total.reshape(8, 32, 256)
            rows = pl.ds(pl.multiple_of(by * 128, 128), 128)
            cols = pl.ds(pl.multiple_of(b * 128, 128), 128)
            tmp[0] = var[0, rows, cols].astype(F32)
            vs = block_tiles(tmp, 0)
            row0 = pl.multiple_of(by * 8, 8)
            for c in range(1, CHUNKS):
                weight = 1.0 / jnp.concatenate(vs[2 * c : 2 * c + 2], axis=0)
                got = jnp.concatenate(
                    [wide[2 * c + j, pl.ds(row0, 8), :] for j in range(2)], axis=0
                )
                free[c - 1, k, pl.ds(0, 16)] = (got * weight).astype(BF16)
                free[c - 1, k, pl.ds(16, 16)] = weight.astype(BF16)

    @pl.when(cell == cells - 1)
    def _():
        copy = pltpu.make_async_copy(codes, out.at[:, pl.ds(ALL * 32, 16)], code_sem)
        copy.start()
        copy.wait()


def other_kernel(dest, tiled, var, coef, bx, ry, *rest):
    outs, rest = rest[: 2 * (CHUNKS - 1)], rest[2 * (CHUNKS - 1) :]
    outs = [outs[2 * i : 2 * i + 2] for i in range(CHUNKS - 1)]
    tiles, src, tmp, rolled, wts, acc, blocks, sems = rest
    cell, cells = pl.program_id(0), pl.num_programs(0)
    slot = lax.rem(cell, 2)

    @pl.when(cell == 0)
    def _():
        clear_edges(tiles, src)

    build_weights(coef, bx, ry, rolled, wts)

    def stack_all(t, _):
        tiles[t, pl.ds(8, 32), :] = tiled[0, t].astype(F32)
        stack_rows(tiles, src, t)
        return 0

    lax.fori_loop(0, 32, stack_all, 0, unroll=4)

    for i in range(CHUNKS - 1):
        convolve(src, wts, acc, i + 1, i)

    @pl.when(cell >= 2)
    def _():
        drain(blocks, outs, sems, slot)

    finish(var, tmp, acc, blocks, slot, list(range(1, CHUNKS)))
    scatter(dest, blocks, outs, sems, cell, cells, slot)


def match_cells(dest, images, variance, coef_rows, band_x, rows_y, codes):
    cells = images.shape[0]
    owners = codes.shape[0]
    out = [
        jax.ShapeDtypeStruct((owners, CAP * 32, 256), BF16),
        jax.ShapeDtypeStruct((owners, EXTRA * 32, 256), BF16),
    ]
    out_codes = jax.ShapeDtypeStruct((owners, ALL * 32 + 16, 256), BF16)
    pixels = pl.BlockSpec((1, 512, 512), lambda i, d: (i, 0, 0))
    tiled_spec = pl.BlockSpec((1, 32, 32, 256), lambda i, d: (i, 0, 0, 0))
    tables = [
        pl.BlockSpec((1, 256, 1), lambda i, d: (i, 0, 0)),
        pl.BlockSpec((48, 256), lambda i, d: (0, 0)),
        pl.BlockSpec((256, 512), lambda i, d: (0, 0)),
    ]
    params = pltpu.CompilerParams(vmem_limit_bytes=48 * 2**20)
    cost = pl.CostEstimate(flops=9000000000, bytes_accessed=30000000, transcendentals=0)

    def scratch(chunks):
        return [
            pltpu.VMEM((32, 48, 256), F32),
            pltpu.VMEM((34, 32, 768), BF16),
            pltpu.VMEM((4, 128, 128), F32),
            pltpu.VMEM((8, 48, 1024), BF16),
            pltpu.VMEM((2304, 256), BF16),
            pltpu.VMEM((chunks, 4, 2, 32, 256), F32),
            pltpu.VMEM((2, chunks, 16, 32, 256), BF16),
            pltpu.SemaphoreType.DMA((2,)),
        ]

    first, tiled, free = pl.pallas_call(
        first_kernel,
        out_shape=[
            out_codes,
            jax.ShapeDtypeStruct((cells, 32, 32, 256), BF16),
            jax.ShapeDtypeStruct((CHUNKS - 1, LOOSE, 32, 256), BF16),
        ],
        grid_spec=pltpu.PrefetchScalarGridSpec(
            num_scalar_prefetch=1,
            grid=(cells,),
            in_specs=[
                pixels,
                pixels,
                *tables,
                pl.BlockSpec((owners, 16, 256), lambda i, d: (0, 0, 0)),
            ],
            out_specs=[
                pl.BlockSpec(memory_space=pl.ANY),
                tiled_spec,
                pl.BlockSpec((CHUNKS - 1, LOOSE, 32, 256), lambda i, d: (0, 0, 0, 0)),
            ],
            scratch_shapes=[
                *scratch(1),
                pltpu.SemaphoreType.DMA,
                pltpu.VMEM((8, 32, 256), F32),
            ],
        ),
        compiler_params=params,
        cost_estimate=cost,
        name="match_first",
    )(dest, images, variance, coef_rows, band_x, rows_y, codes)
    others = pl.pallas_call(
        other_kernel,
        out_shape=out * (CHUNKS - 1),
        grid_spec=pltpu.PrefetchScalarGridSpec(
            num_scalar_prefetch=1,
            grid=(cells,),
            in_specs=[tiled_spec, pixels, *tables],
            out_specs=[pl.BlockSpec(memory_space=pl.ANY)] * (2 * (CHUNKS - 1)),
            scratch_shapes=scratch(CHUNKS - 1),
        ),
        compiler_params=params,
        cost_estimate=cost,
        name="match_others",
    )(dest, tiled, variance, coef_rows, band_x, rows_y)
    return free, [first, *others[0::2]], others[1::2]


def add_kernel(begin, code, group, got, *rest):
    free, outs, acc = rest[:-5], rest[-5:-1], rest[-1]
    step = pl.program_id(0)
    per = got.shape[0]

    @pl.when(step == 0)
    def _():
        acc[...] = jnp.zeros_like(acc)

    def one(i, _):
        at = (step * per + i) * 8
        for r in range(got.shape[1] // 32):
            acc[code[at + begin + r]] += got[i, pl.ds(32 * r, 32), :].astype(F32)
        for r in range(LOOSE if free else 0):
            plane = code[at + ALL + r]

            @pl.when(plane != NONE)
            def _(r=r, plane=plane):
                acc[plane] += free[0][i, pl.ds(32 * r, 32), :].astype(F32)

        return 0

    lax.fori_loop(0, per, one, 0)

    @pl.when(step == pl.num_programs(0) - 1)
    def _():
        def put(p, _):
            for s, out in enumerate(outs):
                share = lax.rem(group[0] + s, 4)
                both = acc[share // 2 * 48 + p]
                fields = both.reshape(2, 16, 256)
                halves = trade_rows(fields[:, :8], fields[:, 8:])
                part = jnp.where(lax.rem(share, 2) == 0, halves[0], halves[1])
                out[p] = part.reshape(16, 256).astype(BF16)
            return 0

        lax.fori_loop(0, 48, put, 0, unroll=2)
        for out in outs:
            out[48] = jnp.full((16, 256), group[1].astype(F32), F32).astype(BF16)


def add_slots(code, group, got, begin, free=None, part=0):
    steps = 2
    per = got.shape[0] // steps
    count = got.shape[1] // 32 * 32
    share = jax.ShapeDtypeStruct((49, 16, 256), BF16)
    specs = [pl.BlockSpec((per, count, 256), lambda i, d, g: (i, 0, 0))]
    if free is not None:
        specs.append(pl.BlockSpec((per, LOOSE * 32, 256), lambda i, d, g: (i, part, 0)))
    return pl.pallas_call(
        functools.partial(add_kernel, begin),
        out_shape=[share] * 4,
        grid_spec=pltpu.PrefetchScalarGridSpec(
            num_scalar_prefetch=2,
            grid=(steps,),
            in_specs=specs,
            out_specs=[pl.BlockSpec((49, 16, 256), lambda i, d, g: (0, 0, 0))] * 4,
            scratch_shapes=[pltpu.VMEM((NONE + 1, 32, 256), F32)],
        ),
        compiler_params=pltpu.CompilerParams(vmem_limit_bytes=48 * 2**20),
        cost_estimate=pl.CostEstimate(flops=6000000, bytes_accessed=6000000, transcendentals=0),
        name="add_slots",
    )(code, group, got, *([] if free is None else [free]))


def ratio_kernel(counts, *refs):
    ins, out, lines = refs[:-2], refs[-2], refs[-1]
    starts = [sum(counts[:c]) for c in range(CHUNKS)]

    def half(qx, _):
        def one(i, _):
            f = i * 2
            vs = []
            for c in range(CHUNKS):
                pair = []
                for k in range(2):
                    total = ins[starts[c]][qx * 6 + f + k].astype(F32)
                    for s in range(1, counts[c]):
                        total += ins[starts[c] + s][qx * 6 + f + k].astype(F32)
                    pair.append(total[:8] / jnp.maximum(total[8:], 1.0))
                vs.extend(trade_rows(*pair))
            for h in range(2):
                got = trade_groups([v[:, 128 * h : 128 * h + 128] for v in vs])
                for k, line in enumerate(got):
                    lines[pl.ds(f * 64 + 8 * h + k, 8, stride=16), :] = line
            return 0

        lax.fori_loop(0, 3, one, 0, unroll=3)
        out[0, :, pl.ds(pl.multiple_of(qx * 128, 128), 128)] = lines[...]
        return 0

    lax.fori_loop(0, 2, half, 0)


def ratio(shares):
    counts = [len(share) for share in shares]
    parts = [x for share in shares for x in share]
    patches = parts[0].shape[0] // 12
    out = pl.pallas_call(
        functools.partial(ratio_kernel, counts),
        grid=(patches,),
        out_shape=jax.ShapeDtypeStruct((patches, FILTERS * 64, 256), F32),
        in_specs=[pl.BlockSpec((12, 16, 256), lambda i: (i, 0, 0))] * len(parts),
        out_specs=pl.BlockSpec((1, FILTERS * 64, 256), lambda i: (i, 0, 0)),
        scratch_shapes=[pltpu.VMEM((FILTERS * 64, 128), F32)],
        compiler_params=pltpu.CompilerParams(vmem_limit_bytes=48 * 2**20),
        name="ratio",
    )(*parts)
    return out.reshape(patches, FILTERS, 64, 256)


def tap_tables(kernel_x, kernel_y):
    jx = jnp.arange(48)[:, None]
    ix = jnp.arange(16)[None, :]
    pick = ((jx - ix - 6)[None] == jnp.arange(TAPS)[:, None, None]).astype(BF16)
    band_x = jnp.einsum("kt,tji->jki", kernel_x, pick, preferred_element_type=F32)
    band_x = band_x.astype(BF16).reshape(48, BASIS * 16)
    line = jnp.arange(512)
    tap = jnp.arange(TAPS)
    pick_y = (41 - (line // 16 + 16)[None, :] == tap[:, None]).astype(BF16)
    taps_y = jnp.dot(kernel_y, pick_y, preferred_element_type=F32).astype(BF16)
    row = jnp.arange(BASIS * 16)
    spread = (row[:, None] // 16 == jnp.arange(BASIS)[None, :]).astype(BF16)
    rows_y = jnp.dot(spread, taps_y, preferred_element_type=F32)
    rows_y = jnp.where(row[:, None] % 16 == line[None, :] % 16, rows_y, 0.0)
    return band_x, rows_y


def exchange(planes, groups):
    moved = [planes[0]]
    for s in range(1, groups):
        ring = [(i, (i + s) % groups) for i in range(groups)]
        moved.append(lax.ppermute(planes[s], "exp", ring))
    return moved


def on_device(images, variance, kernel_x, kernel_y, coef, exposure_filter, block_patch, patch_home):
    cell_count = images.shape[0]
    owner_count = lax.axis_size("patch")
    patches_local = patch_home.shape[0] // owner_count
    block_count = cell_count * 16

    targets = block_patch.reshape(-1)
    patch_index = targets // 4
    quadrant = targets % 4
    home_slot = jnp.sum(
        jnp.where(
            patch_index[:, None] == jnp.arange(patch_home.shape[0])[None, :], patch_home[None, :], 0
        ),
        axis=1,
    )
    owner_index = home_slot // patches_local
    local_patch = home_slot % patches_local
    band_index = jnp.repeat(exposure_filter, 16)
    order = jnp.arange(block_count)
    earlier = order[None, :] < order[:, None]
    rank = jnp.sum((owner_index[:, None] == owner_index[None, :]) & earlier, axis=1)
    late = rank >= CAP
    late_rank = jnp.sum(late[None, :] & earlier, axis=1)
    loose = late & (late_rank < LOOSE)
    more = jnp.any(late & (late_rank >= LOOSE))
    which = loose & (late_rank == jnp.arange(LOOSE)[:, None])
    which = jnp.max(jnp.where(which, order, -16), axis=1)
    dest = jnp.concatenate([owner_index * 8 + rank, which]).astype(jnp.int32)
    code = (
        (quadrant // 2) * 48 + (local_patch * 2 + quadrant % 2) * FILTERS + band_index
    )
    place = jnp.where(loose, ALL + late_rank, -1)
    more_place = jnp.where(late & ~loose, rank, -1)
    owners = jnp.arange(owner_count)[:, None, None]
    row = jnp.arange(16)[:, None]
    here = (rank == row) | (place == row) | (more_place + 5 == row) & (row >= 9)
    codes = jnp.min(jnp.where((owner_index == owners) & here, code, NONE), axis=2)
    codes = jnp.where(jnp.arange(16) == 8, more.astype(code.dtype), codes)
    codes = jnp.pad(codes.astype(BF16)[:, None, :], ((0, 0), (0, 15), (0, 240)))

    band_x, rows_y = tap_tables(kernel_x, kernel_y)
    coef_rows = jnp.repeat(coef, 16, axis=1)[:, :, None]
    free, mains, extras = match_cells(dest, images, variance, coef_rows, band_x, rows_y, codes)

    groups = lax.axis_size("exp")
    def send(part):
        return lax.all_to_all(part, "patch", 0, 0, tiled=True)

    gathered = lax.all_gather(free.reshape(-1, 256), "patch")
    got_0 = send(mains[0])
    head = got_0[:, ALL * 32, :16].astype(jnp.int32)
    got_code = head[:, :8].reshape(-1)
    group = jnp.stack([lax.axis_index("exp"), jnp.max(head[:, 8])])

    def add(got, c):
        return add_slots(got_code, group, got, 0, gathered, c - 1)

    hold = lax.optimization_barrier
    planes_0 = add_slots(got_code, group, got_0, 0)
    share_0 = exchange(planes_0, groups)
    got_1 = send(mains[1])
    part_2, own = hold((mains[2], planes_0[0]))
    share_0[0] = own
    planes_1 = add(got_1, 1)
    share_1 = exchange(planes_1, groups)
    got_2 = send(part_2)
    part_3, share_0, share_1[0] = hold((mains[3], share_0, share_1[0]))
    share_2 = exchange(add(got_2, 2), groups)
    got_3, share_1 = hold((send(part_3), share_1))
    share_3 = exchange(add(got_3, 3), groups)
    shares = [share_0, share_1, share_2, share_3]

    def plain(shares, extras, head):
        return ratio(shares)

    def with_more(shares, extras, head):
        codes = jnp.concatenate([head[:, :CAP], head[:, 9 : 9 + EXTRA], head[:, :2]], axis=1)
        parts = [shares[0]]
        for share, extra in zip(shares[1:], extras, strict=True):
            planes = add_slots(codes.reshape(-1), group, send(extra), CAP)
            parts.append([*share, *exchange(planes, groups)])
        return ratio(parts)

    more = functools.reduce(jnp.maximum, [x[48, 0, 0] for x in share_0]) > 0
    return lax.cond(more, with_more, plain, shares, extras, head)


def solution(mesh):
    return jax.shard_map(
        on_device,
        mesh=mesh,
        in_specs=(
            P(("exp", "patch"), None, None),
            P(("exp", "patch"), None, None),
            P(),
            P(),
            P(("exp", "patch"), None),
            P(("exp", "patch")),
            P(("exp", "patch"), None),
            P(),
        ),
        out_specs=P("patch", None, "exp", None),
        check_vma=False,
    )
```

```python
import functools

import jax
import jax.numpy as jnp
from jax import lax
from jax.experimental import pallas as pl
from jax.experimental.pallas import tpu as pltpu
from jax.sharding import PartitionSpec as P

FILTERS = 6
TAPS = 21
BASIS = 16
CHUNKS = 4
CAP = 4
EXTRA = 2
ALL = CAP + EXTRA
LOOSE = 2
NONE = 96
BF16 = jnp.bfloat16
F32 = jnp.float32


def trade_groups(vs):
    grp = lax.broadcasted_iota(jnp.int32, vs[0].shape, 1) // 16
    a = [v if i == 0 else pltpu.roll(v, 16 * i, 1) for i, v in enumerate(vs)]
    a = [a[-j % 8] for j in range(8)]
    for s in (1, 2, 4):
        pick = (grp & s) != 0
        a = [jnp.where(pick, a[(j - s) % 8], a[j]) for j in range(8)]
    return [v if j == 0 else pltpu.roll(v, 128 - 16 * j, 1) for j, v in enumerate(a)]


def trade_rows(a, b):
    upper = lax.broadcasted_iota(jnp.int32, a.shape, a.ndim - 2) < 4
    axis = a.ndim - 2
    return (
        jnp.where(upper, a, pltpu.roll(b, 4, axis)),
        jnp.where(upper, pltpu.roll(a, 4, axis), b),
    )


def block_tiles(tmp, b):
    halves = [
        trade_groups([tmp[b, pl.ds(8 * h + i, 8, stride=16), :] for i in range(8)])
        for h in range(2)
    ]
    return [jnp.concatenate([halves[0][j], halves[1][j]], axis=1) for j in range(8)]


def strip_tiles(ref, tmp, by):
    rows = pl.ds(pl.multiple_of(by * 128, 128), 128)
    for b in range(4):
        tmp[b] = ref[0, rows, pl.ds(128 * b, 128)].astype(F32)
    return [block_tiles(tmp, b) for b in range(4)]


def convolve(src, wts, acc, chunk, slot):
    lhs = [
        jnp.concatenate(
            [src[pl.ds(b * 8 + 2 * chunk + dx, 2)].reshape(64, 768) for b in range(4)], axis=0
        )
        for dx in range(3)
    ]
    total = jnp.dot(jnp.concatenate(lhs, axis=1), wts[...], preferred_element_type=F32)
    acc[slot] = total.reshape(4, 2, 32, 256)


def finish(var, tmp, acc, blocks, slot, chunks):
    def block_row(by, _):
        row0 = pl.multiple_of(by * 8, 8)
        for b, vs in enumerate(strip_tiles(var, tmp, by)):
            for i, c in enumerate(chunks):
                weight = 1.0 / jnp.concatenate(vs[2 * c : 2 * c + 2], axis=0)
                got = jnp.concatenate([acc[i, b, j, pl.ds(row0, 8), :] for j in range(2)], axis=0)
                blocks[slot, i, by * 4 + b, pl.ds(0, 16)] = (got * weight).astype(BF16)
                blocks[slot, i, by * 4 + b, pl.ds(16, 16)] = weight.astype(BF16)
        return 0

    lax.fori_loop(0, 4, block_row, 0, unroll=2 if len(chunks) == 1 else 1)


def drain(blocks, outs, sems, slot):
    def one(i, _):
        pltpu.make_async_copy(blocks.at[slot, 0, 0], outs[0][0].at[0, pl.ds(0, 32)], sems.at[slot]).wait()
        return 0

    lax.fori_loop(0, 16 * len(outs), one, 0, unroll=16)


def scatter(dest, blocks, outs, sems, cell, cells, slot):
    def send(b, _):
        where = dest[cell * 16 + b]
        owner, rank = where // 8, lax.rem(where, 8)

        def copy(i, target):
            pltpu.make_async_copy(blocks.at[slot, i, b], target, sems.at[slot]).start()

        def rows(k):
            return pl.ds(pl.multiple_of(k * 32, 32), 32)

        if outs[0][1] is None:
            for i, (main, _) in enumerate(outs):
                copy(i, main.at[owner, rows(rank)])
            return 0

        @pl.when(rank < CAP)
        def _():
            for i, (main, _) in enumerate(outs):
                copy(i, main.at[owner, rows(rank)])

        @pl.when(rank >= CAP)
        def _():
            for i, (_, extra) in enumerate(outs):
                copy(i, extra.at[owner, rows(rank - CAP)])

        return 0

    lax.fori_loop(0, 16, send, 0, unroll=16)

    @pl.when(cell == cells - 1)
    def _():
        drain(blocks, outs, sems, slot)
        drain(blocks, outs, sems, 1 - slot)


def build_weights(coef, bx, ry, rolled, wts):
    scaled = (coef[0] * ry[...]).astype(BF16)
    core = jnp.dot(bx[...], scaled, preferred_element_type=F32)
    side = jnp.zeros((48, 256), F32)
    wide = jnp.concatenate([side, core, side], axis=1)
    for r in range(8):
        turned = wide if r == 0 else pltpu.roll(wide, 1024 - 16 * r, 1)
        rolled[r] = turned.astype(BF16)
    for jy in range(48):
        start = 47 - jy
        r, base = start % 8, start // 8 * 128
        for dx in range(3):
            wts[pl.ds(dx * 768 + jy * 16, 16), :] = rolled[
                r, pl.ds(dx * 16, 16), pl.ds(base, 256)
            ]


def clear_edges(tiles, src):
    tiles[:, 0:8, :] = jnp.zeros((32, 8, 256), F32)
    tiles[:, 40:48, :] = jnp.zeros((32, 8, 256), F32)
    src[0] = jnp.zeros((32, 768), BF16)
    src[33] = jnp.zeros((32, 768), BF16)


def stack_rows(tiles, src, t):
    for dy in range(3):
        src[1 + t, :, pl.ds(dy * 256, 256)] = tiles[t, pl.ds(7 + dy, 32), :].astype(BF16)


def first_kernel(
    dest, img, var, coef, bx, ry, codes, out, tiled, free, *scratch
):
    tiles, src, tmp, rolled, wts, acc, blocks, sems, code_sem, wide = scratch
    cell, cells = pl.program_id(0), pl.num_programs(0)
    slot = lax.rem(cell, 2)

    @pl.when(cell == 0)
    def _():
        clear_edges(tiles, src)

    build_weights(coef, bx, ry, rolled, wts)

    def tile_block(by, _):
        row0 = pl.multiple_of(8 + by * 8, 8)
        for b, vs in enumerate(strip_tiles(img, tmp, by)):
            for j, v in enumerate(vs):
                tiles[b * 8 + j, pl.ds(row0, 8), :] = v
        return 0

    lax.fori_loop(0, 4, tile_block, 0)

    def stack_some(b, _):
        for k in range(3):
            stack_rows(tiles, src, b * 8 + k)

        @pl.when(b > 0)
        def _():
            stack_rows(tiles, src, b * 8 - 1)

        return 0

    lax.fori_loop(0, 4, stack_some, 0, unroll=4)

    def keep(t, _):
        tiled[0, t] = tiles[t, pl.ds(8, 32), :].astype(BF16)
        return 0

    lax.fori_loop(0, 32, keep, 0, unroll=32)

    convolve(src, wts, acc, 0, 0)

    @pl.when(cell >= 2)
    def _():
        drain(blocks, [(out, None)], sems, slot)

    finish(var, tmp, acc, blocks, slot, [0])
    scatter(dest, blocks, [(out, None)], sems, cell, cells, slot)

    for k in range(LOOSE):
        which = dest[cells * 16 + k]

        @pl.when(which // 16 == cell)
        def _(k=k, which=which):
            by, b = lax.rem(which, 16) // 4, lax.rem(which, 4)
            for j in range(3, 8):
                stack_rows(tiles, src, b * 8 + j)
            lhs = [src[pl.ds(b * 8 + dx, 8)].reshape(256, 768) for dx in range(3)]
            total = jnp.dot(
                jnp.concatenate(lhs, axis=1), wts[...], preferred_element_type=F32
            )
            wide[...] = total.reshape(8, 32, 256)
            rows = pl.ds(pl.multiple_of(by * 128, 128), 128)
            cols = pl.ds(pl.multiple_of(b * 128, 128), 128)
            tmp[0] = var[0, rows, cols].astype(F32)
            vs = block_tiles(tmp, 0)
            row0 = pl.multiple_of(by * 8, 8)
            for c in range(1, CHUNKS):
                weight = 1.0 / jnp.concatenate(vs[2 * c : 2 * c + 2], axis=0)
                got = jnp.concatenate(
                    [wide[2 * c + j, pl.ds(row0, 8), :] for j in range(2)], axis=0
                )
                free[c - 1, k, pl.ds(0, 16)] = (got * weight).astype(BF16)
                free[c - 1, k, pl.ds(16, 16)] = weight.astype(BF16)

    @pl.when(cell == cells - 1)
    def _():
        copy = pltpu.make_async_copy(codes, out.at[:, pl.ds(ALL * 32, 16)], code_sem)
        copy.start()
        copy.wait()


def other_kernel(dest, tiled, var, coef, bx, ry, *rest):
    outs, rest = rest[: 2 * (CHUNKS - 1)], rest[2 * (CHUNKS - 1) :]
    outs = [outs[2 * i : 2 * i + 2] for i in range(CHUNKS - 1)]
    tiles, src, tmp, rolled, wts, acc, blocks, sems = rest
    cell, cells = pl.program_id(0), pl.num_programs(0)
    slot = lax.rem(cell, 2)

    @pl.when(cell == 0)
    def _():
        clear_edges(tiles, src)

    build_weights(coef, bx, ry, rolled, wts)

    def stack_all(t, _):
        tiles[t, pl.ds(8, 32), :] = tiled[0, t].astype(F32)
        stack_rows(tiles, src, t)
        return 0

    lax.fori_loop(0, 32, stack_all, 0, unroll=8)

    for i in range(CHUNKS - 1):
        convolve(src, wts, acc, i + 1, i)

    @pl.when(cell >= 2)
    def _():
        drain(blocks, outs, sems, slot)

    finish(var, tmp, acc, blocks, slot, list(range(1, CHUNKS)))
    scatter(dest, blocks, outs, sems, cell, cells, slot)


def match_cells(dest, images, variance, coef_rows, band_x, rows_y, codes):
    cells = images.shape[0]
    owners = codes.shape[0]
    out = [
        jax.ShapeDtypeStruct((owners, CAP * 32, 256), BF16),
        jax.ShapeDtypeStruct((owners, EXTRA * 32, 256), BF16),
    ]
    out_codes = jax.ShapeDtypeStruct((owners, ALL * 32 + 16, 256), BF16)
    pixels = pl.BlockSpec((1, 512, 512), lambda i, d: (i, 0, 0))
    tiled_spec = pl.BlockSpec((1, 32, 32, 256), lambda i, d: (i, 0, 0, 0))
    tables = [
        pl.BlockSpec((1, 256, 1), lambda i, d: (i, 0, 0)),
        pl.BlockSpec((48, 256), lambda i, d: (0, 0)),
        pl.BlockSpec((256, 512), lambda i, d: (0, 0)),
    ]
    params = pltpu.CompilerParams(vmem_limit_bytes=48 * 2**20)
    cost = pl.CostEstimate(flops=9000000000, bytes_accessed=30000000, transcendentals=0)

    def scratch(chunks):
        return [
            pltpu.VMEM((32, 48, 256), F32),
            pltpu.VMEM((34, 32, 768), BF16),
            pltpu.VMEM((4, 128, 128), F32),
            pltpu.VMEM((8, 48, 1024), BF16),
            pltpu.VMEM((2304, 256), BF16),
            pltpu.VMEM((chunks, 4, 2, 32, 256), F32),
            pltpu.VMEM((2, chunks, 16, 32, 256), BF16),
            pltpu.SemaphoreType.DMA((2,)),
        ]

    first, tiled, free = pl.pallas_call(
        first_kernel,
        out_shape=[
            out_codes,
            jax.ShapeDtypeStruct((cells, 32, 32, 256), BF16),
            jax.ShapeDtypeStruct((CHUNKS - 1, LOOSE, 32, 256), BF16),
        ],
        grid_spec=pltpu.PrefetchScalarGridSpec(
            num_scalar_prefetch=1,
            grid=(cells,),
            in_specs=[
                pixels,
                pixels,
                *tables,
                pl.BlockSpec((owners, 16, 256), lambda i, d: (0, 0, 0)),
            ],
            out_specs=[
                pl.BlockSpec(memory_space=pl.ANY),
                tiled_spec,
                pl.BlockSpec((CHUNKS - 1, LOOSE, 32, 256), lambda i, d: (0, 0, 0, 0)),
            ],
            scratch_shapes=[
                *scratch(1),
                pltpu.SemaphoreType.DMA,
                pltpu.VMEM((8, 32, 256), F32),
            ],
        ),
        compiler_params=params,
        cost_estimate=cost,
        name="match_first",
    )(dest, images, variance, coef_rows, band_x, rows_y, codes)
    others = pl.pallas_call(
        other_kernel,
        out_shape=out * (CHUNKS - 1),
        grid_spec=pltpu.PrefetchScalarGridSpec(
            num_scalar_prefetch=1,
            grid=(cells,),
            in_specs=[tiled_spec, pixels, *tables],
            out_specs=[pl.BlockSpec(memory_space=pl.ANY)] * (2 * (CHUNKS - 1)),
            scratch_shapes=scratch(CHUNKS - 1),
        ),
        compiler_params=params,
        cost_estimate=cost,
        name="match_others",
    )(dest, tiled, variance, coef_rows, band_x, rows_y)
    return free, [first, *others[0::2]], others[1::2]


def add_kernel(begin, code, group, got, *rest):
    free, outs, acc = rest[:-5], rest[-5:-1], rest[-1]
    step = pl.program_id(0)
    per = got.shape[0]

    @pl.when(step == 0)
    def _():
        acc[...] = jnp.zeros_like(acc)

    def one(i, _):
        at = (step * per + i) * 8
        for r in range(got.shape[1] // 32):
            acc[code[at + begin + r]] += got[i, pl.ds(32 * r, 32), :].astype(F32)
        for r in range(LOOSE if free else 0):
            plane = code[at + ALL + r]

            @pl.when(plane != NONE)
            def _(r=r, plane=plane):
                acc[plane] += free[0][i, pl.ds(32 * r, 32), :].astype(F32)

        return 0

    lax.fori_loop(0, per, one, 0)

    @pl.when(step == pl.num_programs(0) - 1)
    def _():
        def put(p, _):
            for s, out in enumerate(outs):
                share = lax.rem(group[0] + s, 4)
                both = acc[share // 2 * 48 + p]
                fields = both.reshape(2, 16, 256)
                halves = trade_rows(fields[:, :8], fields[:, 8:])
                part = jnp.where(lax.rem(share, 2) == 0, halves[0], halves[1])
                out[p] = part.reshape(16, 256).astype(BF16)
            return 0

        lax.fori_loop(0, 48, put, 0, unroll=2)
        for out in outs:
            out[48] = jnp.full((16, 256), group[1].astype(F32), F32).astype(BF16)


def add_slots(code, group, got, begin, free=None, part=0):
    steps = 2
    per = got.shape[0] // steps
    count = got.shape[1] // 32 * 32
    share = jax.ShapeDtypeStruct((49, 16, 256), BF16)
    specs = [pl.BlockSpec((per, count, 256), lambda i, d, g: (i, 0, 0))]
    if free is not None:
        specs.append(pl.BlockSpec((per, LOOSE * 32, 256), lambda i, d, g: (i, part, 0)))
    return pl.pallas_call(
        functools.partial(add_kernel, begin),
        out_shape=[share] * 4,
        grid_spec=pltpu.PrefetchScalarGridSpec(
            num_scalar_prefetch=2,
            grid=(steps,),
            in_specs=specs,
            out_specs=[pl.BlockSpec((49, 16, 256), lambda i, d, g: (0, 0, 0))] * 4,
            scratch_shapes=[pltpu.VMEM((NONE + 1, 32, 256), F32)],
        ),
        compiler_params=pltpu.CompilerParams(vmem_limit_bytes=48 * 2**20),
        cost_estimate=pl.CostEstimate(flops=6000000, bytes_accessed=6000000, transcendentals=0),
        name="add_slots",
    )(code, group, got, *([] if free is None else [free]))


def ratio_kernel(counts, *refs):
    ins, out, lines = refs[:-2], refs[-2], refs[-1]
    starts = [sum(counts[:c]) for c in range(CHUNKS)]

    def half(qx, _):
        def one(i, _):
            f = i * 2
            vs = []
            for c in range(CHUNKS):
                pair = []
                for k in range(2):
                    total = ins[starts[c]][qx * 6 + f + k].astype(F32)
                    for s in range(1, counts[c]):
                        total += ins[starts[c] + s][qx * 6 + f + k].astype(F32)
                    pair.append(total[:8] / jnp.maximum(total[8:], 1.0))
                vs.extend(trade_rows(*pair))
            for h in range(2):
                got = trade_groups([v[:, 128 * h : 128 * h + 128] for v in vs])
                for k, line in enumerate(got):
                    lines[pl.ds(f * 64 + 8 * h + k, 8, stride=16), :] = line
            return 0

        lax.fori_loop(0, 3, one, 0, unroll=3)
        out[0, :, pl.ds(pl.multiple_of(qx * 128, 128), 128)] = lines[...]
        return 0

    lax.fori_loop(0, 2, half, 0)


def ratio(shares):
    counts = [len(share) for share in shares]
    parts = [x for share in shares for x in share]
    patches = parts[0].shape[0] // 12
    out = pl.pallas_call(
        functools.partial(ratio_kernel, counts),
        grid=(patches,),
        out_shape=jax.ShapeDtypeStruct((patches, FILTERS * 64, 256), F32),
        in_specs=[pl.BlockSpec((12, 16, 256), lambda i: (i, 0, 0))] * len(parts),
        out_specs=pl.BlockSpec((1, FILTERS * 64, 256), lambda i: (i, 0, 0)),
        scratch_shapes=[pltpu.VMEM((FILTERS * 64, 128), F32)],
        compiler_params=pltpu.CompilerParams(vmem_limit_bytes=48 * 2**20),
        name="ratio",
    )(*parts)
    return out.reshape(patches, FILTERS, 64, 256)


def tap_tables(kernel_x, kernel_y):
    jx = jnp.arange(48)[:, None]
    ix = jnp.arange(16)[None, :]
    pick = ((jx - ix - 6)[None] == jnp.arange(TAPS)[:, None, None]).astype(BF16)
    band_x = jnp.einsum("kt,tji->jki", kernel_x, pick, preferred_element_type=F32)
    band_x = band_x.astype(BF16).reshape(48, BASIS * 16)
    line = jnp.arange(512)
    tap = jnp.arange(TAPS)
    pick_y = (41 - (line // 16 + 16)[None, :] == tap[:, None]).astype(BF16)
    taps_y = jnp.dot(kernel_y, pick_y, preferred_element_type=F32).astype(BF16)
    row = jnp.arange(BASIS * 16)
    spread = (row[:, None] // 16 == jnp.arange(BASIS)[None, :]).astype(BF16)
    rows_y = jnp.dot(spread, taps_y, preferred_element_type=F32)
    rows_y = jnp.where(row[:, None] % 16 == line[None, :] % 16, rows_y, 0.0)
    return band_x, rows_y


def exchange(planes, groups):
    moved = [planes[0]]
    for s in range(1, groups):
        ring = [(i, (i + s) % groups) for i in range(groups)]
        moved.append(lax.ppermute(planes[s], "exp", ring))
    return moved


def on_device(images, variance, kernel_x, kernel_y, coef, exposure_filter, block_patch, patch_home):
    cell_count = images.shape[0]
    owner_count = lax.axis_size("patch")
    patches_local = patch_home.shape[0] // owner_count
    block_count = cell_count * 16

    targets = block_patch.reshape(-1)
    patch_index = targets // 4
    quadrant = targets % 4
    home_slot = jnp.sum(
        jnp.where(
            patch_index[:, None] == jnp.arange(patch_home.shape[0])[None, :], patch_home[None, :], 0
        ),
        axis=1,
    )
    owner_index = home_slot // patches_local
    local_patch = home_slot % patches_local
    band_index = jnp.repeat(exposure_filter, 16)
    order = jnp.arange(block_count)
    earlier = order[None, :] < order[:, None]
    rank = jnp.sum((owner_index[:, None] == owner_index[None, :]) & earlier, axis=1)
    late = rank >= CAP
    late_rank = jnp.sum(late[None, :] & earlier, axis=1)
    loose = late & (late_rank < LOOSE)
    more = jnp.any(late & (late_rank >= LOOSE))
    which = loose & (late_rank == jnp.arange(LOOSE)[:, None])
    which = jnp.max(jnp.where(which, order, -16), axis=1)
    dest = jnp.concatenate([owner_index * 8 + rank, which]).astype(jnp.int32)
    code = (
        (quadrant // 2) * 48 + (local_patch * 2 + quadrant % 2) * FILTERS + band_index
    )
    place = jnp.where(loose, ALL + late_rank, -1)
    more_place = jnp.where(late & ~loose, rank, -1)
    owners = jnp.arange(owner_count)[:, None, None]
    row = jnp.arange(16)[:, None]
    here = (rank == row) | (place == row) | (more_place + 5 == row) & (row >= 9)
    codes = jnp.min(jnp.where((owner_index == owners) & here, code, NONE), axis=2)
    codes = jnp.where(jnp.arange(16) == 8, more.astype(code.dtype), codes)
    codes = jnp.pad(codes.astype(BF16)[:, None, :], ((0, 0), (0, 15), (0, 240)))

    band_x, rows_y = tap_tables(kernel_x, kernel_y)
    coef_rows = jnp.repeat(coef, 16, axis=1)[:, :, None]
    free, mains, extras = match_cells(dest, images, variance, coef_rows, band_x, rows_y, codes)

    groups = lax.axis_size("exp")
    def send(part):
        return lax.all_to_all(part, "patch", 0, 0, tiled=True)

    gathered = lax.all_gather(free.reshape(-1, 256), "patch")
    got_0 = send(mains[0])
    head = got_0[:, ALL * 32, :16].astype(jnp.int32)
    got_code = head[:, :8].reshape(-1)
    group = jnp.stack([lax.axis_index("exp"), jnp.max(head[:, 8])])

    def add(got, c):
        return add_slots(got_code, group, got, 0, gathered, c - 1)

    hold = lax.optimization_barrier
    planes_0 = add_slots(got_code, group, got_0, 0)
    share_0 = exchange(planes_0, groups)
    got_1 = send(mains[1])
    part_2, own = hold((mains[2], planes_0[0]))
    share_0[0] = own
    planes_1 = add(got_1, 1)
    share_1 = exchange(planes_1, groups)
    got_2 = send(part_2)
    part_3, share_0, share_1[0] = hold((mains[3], share_0, share_1[0]))
    share_2 = exchange(add(got_2, 2), groups)
    got_3, share_1 = hold((send(part_3), share_1))
    share_3 = exchange(add(got_3, 3), groups)
    shares = [share_0, share_1, share_2, share_3]

    def plain(shares, extras, head):
        return ratio(shares)

    def with_more(shares, extras, head):
        codes = jnp.concatenate([head[:, :CAP], head[:, 9 : 9 + EXTRA], head[:, :2]], axis=1)
        parts = [shares[0]]
        for share, extra in zip(shares[1:], extras, strict=True):
            planes = add_slots(codes.reshape(-1), group, send(extra), CAP)
            parts.append([*share, *exchange(planes, groups)])
        return ratio(parts)

    more = functools.reduce(jnp.maximum, [x[48, 0, 0] for x in share_0]) > 0
    return lax.cond(more, with_more, plain, shares, extras, head)


def solution(mesh):
    return jax.shard_map(
        on_device,
        mesh=mesh,
        in_specs=(
            P(("exp", "patch"), None, None),
            P(("exp", "patch"), None, None),
            P(),
            P(),
            P(("exp", "patch"), None),
            P(("exp", "patch")),
            P(("exp", "patch"), None),
            P(),
        ),
        out_specs=P("patch", None, "exp", None),
        check_vma=False,
    )
```

```python
import functools

import jax
import jax.numpy as jnp
from jax import lax
from jax.experimental import pallas as pl
from jax.experimental.pallas import tpu as pltpu
from jax.sharding import PartitionSpec as P

FILTERS = 6
TAPS = 21
BASIS = 16
CHUNKS = 4
CAP = 4
EXTRA = 2
ALL = CAP + EXTRA
LOOSE = 2
NONE = 96
BF16 = jnp.bfloat16
F32 = jnp.float32


def trade_groups(vs):
    grp = lax.broadcasted_iota(jnp.int32, vs[0].shape, 1) // 16
    a = [v if i == 0 else pltpu.roll(v, 16 * i, 1) for i, v in enumerate(vs)]
    a = [a[-j % 8] for j in range(8)]
    for s in (1, 2, 4):
        pick = (grp & s) != 0
        a = [jnp.where(pick, a[(j - s) % 8], a[j]) for j in range(8)]
    return [v if j == 0 else pltpu.roll(v, 128 - 16 * j, 1) for j, v in enumerate(a)]


def trade_rows(a, b):
    upper = lax.broadcasted_iota(jnp.int32, a.shape, a.ndim - 2) < 4
    axis = a.ndim - 2
    return (
        jnp.where(upper, a, pltpu.roll(b, 4, axis)),
        jnp.where(upper, pltpu.roll(a, 4, axis), b),
    )


def block_tiles(tmp, b):
    halves = [
        trade_groups([tmp[b, pl.ds(8 * h + i, 8, stride=16), :] for i in range(8)])
        for h in range(2)
    ]
    return [jnp.concatenate([halves[0][j], halves[1][j]], axis=1) for j in range(8)]


def strip_tiles(ref, tmp, by):
    rows = pl.ds(pl.multiple_of(by * 128, 128), 128)
    for b in range(4):
        tmp[b] = ref[0, rows, pl.ds(128 * b, 128)].astype(F32)
    return [block_tiles(tmp, b) for b in range(4)]


def convolve(src, wts, acc, chunk, slot):
    lhs = [
        jnp.concatenate(
            [src[pl.ds(b * 8 + 2 * chunk + dx, 2)].reshape(64, 768) for b in range(4)], axis=0
        )
        for dx in range(3)
    ]
    total = jnp.dot(jnp.concatenate(lhs, axis=1), wts[...], preferred_element_type=F32)
    acc[slot] = total.reshape(4, 2, 32, 256)


def finish(var, tmp, acc, blocks, slot, chunks):
    def block_row(by, _):
        row0 = pl.multiple_of(by * 8, 8)
        for b, vs in enumerate(strip_tiles(var, tmp, by)):
            for i, c in enumerate(chunks):
                weight = 1.0 / jnp.concatenate(vs[2 * c : 2 * c + 2], axis=0)
                got = jnp.concatenate([acc[i, b, j, pl.ds(row0, 8), :] for j in range(2)], axis=0)
                blocks[slot, i, by * 4 + b, pl.ds(0, 16)] = (got * weight).astype(BF16)
                blocks[slot, i, by * 4 + b, pl.ds(16, 16)] = weight.astype(BF16)
        return 0

    lax.fori_loop(0, 4, block_row, 0, unroll=2 if len(chunks) == 1 else 1)


def drain(blocks, outs, sems, slot):
    def one(i, _):
        pltpu.make_async_copy(blocks.at[slot, 0, 0], outs[0][0].at[0, pl.ds(0, 32)], sems.at[slot]).wait()
        return 0

    lax.fori_loop(0, 16 * len(outs), one, 0, unroll=16)


def scatter(dest, blocks, outs, sems, cell, cells, slot):
    def send(b, _):
        where = dest[cell * 16 + b]
        owner, rank = where // 8, lax.rem(where, 8)

        def copy(i, target):
            pltpu.make_async_copy(blocks.at[slot, i, b], target, sems.at[slot]).start()

        def rows(k):
            return pl.ds(pl.multiple_of(k * 32, 32), 32)

        if outs[0][1] is None:
            for i, (main, _) in enumerate(outs):
                copy(i, main.at[owner, rows(rank)])
            return 0

        @pl.when(rank < CAP)
        def _():
            for i, (main, _) in enumerate(outs):
                copy(i, main.at[owner, rows(rank)])

        @pl.when(rank >= CAP)
        def _():
            for i, (_, extra) in enumerate(outs):
                copy(i, extra.at[owner, rows(rank - CAP)])

        return 0

    lax.fori_loop(0, 16, send, 0, unroll=16)

    @pl.when(cell == cells - 1)
    def _():
        drain(blocks, outs, sems, slot)
        drain(blocks, outs, sems, 1 - slot)


def build_weights(coef, bx, ry, rolled, wts):
    scaled = (coef[0] * ry[...]).astype(BF16)
    core = jnp.dot(bx[...], scaled, preferred_element_type=F32)
    side = jnp.zeros((48, 256), F32)
    wide = jnp.concatenate([side, core, side], axis=1)
    for r in range(8):
        turned = wide if r == 0 else pltpu.roll(wide, 1024 - 16 * r, 1)
        rolled[r] = turned.astype(BF16)
    for jy in range(48):
        start = 47 - jy
        r, base = start % 8, start // 8 * 128
        for dx in range(3):
            wts[pl.ds(dx * 768 + jy * 16, 16), :] = rolled[
                r, pl.ds(dx * 16, 16), pl.ds(base, 256)
            ]


def clear_edges(tiles, src):
    tiles[:, 0:8, :] = jnp.zeros((32, 8, 256), F32)
    tiles[:, 40:48, :] = jnp.zeros((32, 8, 256), F32)
    src[0] = jnp.zeros((32, 768), BF16)
    src[33] = jnp.zeros((32, 768), BF16)


def stack_rows(tiles, src, t):
    for dy in range(3):
        src[1 + t, :, pl.ds(dy * 256, 256)] = tiles[t, pl.ds(7 + dy, 32), :].astype(BF16)


def first_kernel(
    dest, img, var, coef, bx, ry, codes, out, tiled, free, *scratch
):
    tiles, src, tmp, rolled, wts, acc, blocks, sems, code_sem, wide = scratch
    cell, cells = pl.program_id(0), pl.num_programs(0)
    slot = lax.rem(cell, 2)

    @pl.when(cell == 0)
    def _():
        clear_edges(tiles, src)

    build_weights(coef, bx, ry, rolled, wts)

    def tile_block(by, _):
        row0 = pl.multiple_of(8 + by * 8, 8)
        for b, vs in enumerate(strip_tiles(img, tmp, by)):
            for j, v in enumerate(vs):
                tiles[b * 8 + j, pl.ds(row0, 8), :] = v
        return 0

    lax.fori_loop(0, 4, tile_block, 0)

    def stack_some(b, _):
        for k in range(3):
            stack_rows(tiles, src, b * 8 + k)

        @pl.when(b > 0)
        def _():
            stack_rows(tiles, src, b * 8 - 1)

        return 0

    lax.fori_loop(0, 4, stack_some, 0, unroll=4)

    def keep(t, _):
        tiled[0, t] = tiles[t, pl.ds(8, 32), :].astype(BF16)
        return 0

    lax.fori_loop(0, 32, keep, 0, unroll=32)

    convolve(src, wts, acc, 0, 0)

    @pl.when(cell >= 2)
    def _():
        drain(blocks, [(out, None)], sems, slot)

    finish(var, tmp, acc, blocks, slot, [0])
    scatter(dest, blocks, [(out, None)], sems, cell, cells, slot)

    for k in range(LOOSE):
        which = dest[cells * 16 + k]

        @pl.when(which // 16 == cell)
        def _(k=k, which=which):
            by, b = lax.rem(which, 16) // 4, lax.rem(which, 4)
            for j in range(3, 8):
                stack_rows(tiles, src, b * 8 + j)
            lhs = [src[pl.ds(b * 8 + dx, 8)].reshape(256, 768) for dx in range(3)]
            total = jnp.dot(
                jnp.concatenate(lhs, axis=1), wts[...], preferred_element_type=F32
            )
            wide[...] = total.reshape(8, 32, 256)
            rows = pl.ds(pl.multiple_of(by * 128, 128), 128)
            cols = pl.ds(pl.multiple_of(b * 128, 128), 128)
            tmp[0] = var[0, rows, cols].astype(F32)
            vs = block_tiles(tmp, 0)
            row0 = pl.multiple_of(by * 8, 8)
            for c in range(1, CHUNKS):
                weight = 1.0 / jnp.concatenate(vs[2 * c : 2 * c + 2], axis=0)
                got = jnp.concatenate(
                    [wide[2 * c + j, pl.ds(row0, 8), :] for j in range(2)], axis=0
                )
                free[c - 1, k, pl.ds(0, 16)] = (got * weight).astype(BF16)
                free[c - 1, k, pl.ds(16, 16)] = weight.astype(BF16)

    @pl.when(cell == cells - 1)
    def _():
        copy = pltpu.make_async_copy(codes, out.at[:, pl.ds(ALL * 32, 16)], code_sem)
        copy.start()
        copy.wait()


def other_kernel(dest, tiled, var, coef, bx, ry, *rest):
    outs, rest = rest[: 2 * (CHUNKS - 1)], rest[2 * (CHUNKS - 1) :]
    outs = [outs[2 * i : 2 * i + 2] for i in range(CHUNKS - 1)]
    tiles, src, tmp, rolled, wts, acc, blocks, sems = rest
    cell, cells = pl.program_id(0), pl.num_programs(0)
    slot = lax.rem(cell, 2)

    @pl.when(cell == 0)
    def _():
        clear_edges(tiles, src)

    build_weights(coef, bx, ry, rolled, wts)

    def stack_all(t, _):
        tiles[t, pl.ds(8, 32), :] = tiled[0, t].astype(F32)
        stack_rows(tiles, src, t)
        return 0

    lax.fori_loop(0, 32, stack_all, 0, unroll=8)

    for i in range(CHUNKS - 1):
        convolve(src, wts, acc, i + 1, i)

    @pl.when(cell >= 2)
    def _():
        drain(blocks, outs, sems, slot)

    finish(var, tmp, acc, blocks, slot, list(range(1, CHUNKS)))
    scatter(dest, blocks, outs, sems, cell, cells, slot)


def match_cells(dest, images, variance, coef_rows, band_x, rows_y, codes):
    cells = images.shape[0]
    owners = codes.shape[0]
    out = [
        jax.ShapeDtypeStruct((owners, CAP * 32, 256), BF16),
        jax.ShapeDtypeStruct((owners, EXTRA * 32, 256), BF16),
    ]
    out_codes = jax.ShapeDtypeStruct((owners, ALL * 32 + 16, 256), BF16)
    pixels = pl.BlockSpec((1, 512, 512), lambda i, d: (i, 0, 0))
    tiled_spec = pl.BlockSpec((1, 32, 32, 256), lambda i, d: (i, 0, 0, 0))
    tables = [
        pl.BlockSpec((1, 256, 1), lambda i, d: (i, 0, 0)),
        pl.BlockSpec((48, 256), lambda i, d: (0, 0)),
        pl.BlockSpec((256, 512), lambda i, d: (0, 0)),
    ]
    params = pltpu.CompilerParams(vmem_limit_bytes=48 * 2**20)
    cost = pl.CostEstimate(flops=9000000000, bytes_accessed=30000000, transcendentals=0)

    def scratch(chunks):
        return [
            pltpu.VMEM((32, 48, 256), F32),
            pltpu.VMEM((34, 32, 768), BF16),
            pltpu.VMEM((4, 128, 128), F32),
            pltpu.VMEM((8, 48, 1024), BF16),
            pltpu.VMEM((2304, 256), BF16),
            pltpu.VMEM((chunks, 4, 2, 32, 256), F32),
            pltpu.VMEM((2, chunks, 16, 32, 256), BF16),
            pltpu.SemaphoreType.DMA((2,)),
        ]

    first, tiled, free = pl.pallas_call(
        first_kernel,
        out_shape=[
            out_codes,
            jax.ShapeDtypeStruct((cells, 32, 32, 256), BF16),
            jax.ShapeDtypeStruct((CHUNKS - 1, LOOSE, 32, 256), BF16),
        ],
        grid_spec=pltpu.PrefetchScalarGridSpec(
            num_scalar_prefetch=1,
            grid=(cells,),
            in_specs=[
                pixels,
                pixels,
                *tables,
                pl.BlockSpec((owners, 16, 256), lambda i, d: (0, 0, 0)),
            ],
            out_specs=[
                pl.BlockSpec(memory_space=pl.ANY),
                tiled_spec,
                pl.BlockSpec((CHUNKS - 1, LOOSE, 32, 256), lambda i, d: (0, 0, 0, 0)),
            ],
            scratch_shapes=[
                *scratch(1),
                pltpu.SemaphoreType.DMA,
                pltpu.VMEM((8, 32, 256), F32),
            ],
        ),
        compiler_params=params,
        cost_estimate=cost,
        name="match_first",
    )(dest, images, variance, coef_rows, band_x, rows_y, codes)
    others = pl.pallas_call(
        other_kernel,
        out_shape=out * (CHUNKS - 1),
        grid_spec=pltpu.PrefetchScalarGridSpec(
            num_scalar_prefetch=1,
            grid=(cells,),
            in_specs=[tiled_spec, pixels, *tables],
            out_specs=[pl.BlockSpec(memory_space=pl.ANY)] * (2 * (CHUNKS - 1)),
            scratch_shapes=scratch(CHUNKS - 1),
        ),
        compiler_params=params,
        cost_estimate=cost,
        name="match_others",
    )(dest, tiled, variance, coef_rows, band_x, rows_y)
    return free, [first, *others[0::2]], others[1::2]


def add_kernel(begin, code, group, got, *rest):
    free, outs, acc = rest[:-5], rest[-5:-1], rest[-1]
    step = pl.program_id(0)
    per = got.shape[0]

    @pl.when(step == 0)
    def _():
        acc[...] = jnp.zeros_like(acc)

    def one(i, _):
        at = (step * per + i) * 8
        for r in range(got.shape[1] // 32):
            acc[code[at + begin + r]] += got[i, pl.ds(32 * r, 32), :].astype(F32)
        for r in range(LOOSE if free else 0):
            plane = code[at + ALL + r]

            @pl.when(plane != NONE)
            def _(r=r, plane=plane):
                acc[plane] += free[0][i, pl.ds(32 * r, 32), :].astype(F32)

        return 0

    lax.fori_loop(0, per, one, 0, unroll=2)

    @pl.when(step == pl.num_programs(0) - 1)
    def _():
        def put(p, _):
            for s, out in enumerate(outs):
                share = lax.rem(group[0] + s, 4)
                both = acc[share // 2 * 48 + p]
                fields = both.reshape(2, 16, 256)
                halves = trade_rows(fields[:, :8], fields[:, 8:])
                part = jnp.where(lax.rem(share, 2) == 0, halves[0], halves[1])
                out[p] = part.reshape(16, 256).astype(BF16)
            return 0

        lax.fori_loop(0, 48, put, 0, unroll=4)
        for out in outs:
            out[48] = jnp.full((16, 256), group[1].astype(F32), F32).astype(BF16)


def add_slots(code, group, got, begin, free=None, part=0):
    steps = 2
    per = got.shape[0] // steps
    count = got.shape[1] // 32 * 32
    share = jax.ShapeDtypeStruct((49, 16, 256), BF16)
    specs = [pl.BlockSpec((per, count, 256), lambda i, d, g: (i, 0, 0))]
    if free is not None:
        specs.append(pl.BlockSpec((per, LOOSE * 32, 256), lambda i, d, g: (i, part, 0)))
    return pl.pallas_call(
        functools.partial(add_kernel, begin),
        out_shape=[share] * 4,
        grid_spec=pltpu.PrefetchScalarGridSpec(
            num_scalar_prefetch=2,
            grid=(steps,),
            in_specs=specs,
            out_specs=[pl.BlockSpec((49, 16, 256), lambda i, d, g: (0, 0, 0))] * 4,
            scratch_shapes=[pltpu.VMEM((NONE + 1, 32, 256), F32)],
        ),
        compiler_params=pltpu.CompilerParams(vmem_limit_bytes=48 * 2**20),
        cost_estimate=pl.CostEstimate(flops=6000000, bytes_accessed=6000000, transcendentals=0),
        name="add_slots",
    )(code, group, got, *([] if free is None else [free]))


def ratio_kernel(counts, *refs):
    ins, out, lines = refs[:-2], refs[-2], refs[-1]
    starts = [sum(counts[:c]) for c in range(CHUNKS)]

    def half(qx, _):
        def one(i, _):
            f = i * 2
            vs = []
            for c in range(CHUNKS):
                pair = []
                for k in range(2):
                    total = ins[starts[c]][qx * 6 + f + k].astype(F32)
                    for s in range(1, counts[c]):
                        total += ins[starts[c] + s][qx * 6 + f + k].astype(F32)
                    pair.append(total[:8] / jnp.maximum(total[8:], 1.0))
                vs.extend(trade_rows(*pair))
            for h in range(2):
                got = trade_groups([v[:, 128 * h : 128 * h + 128] for v in vs])
                for k, line in enumerate(got):
                    lines[pl.ds(f * 64 + 8 * h + k, 8, stride=16), :] = line
            return 0

        lax.fori_loop(0, 3, one, 0, unroll=3)
        out[0, :, pl.ds(pl.multiple_of(qx * 128, 128), 128)] = lines[...]
        return 0

    lax.fori_loop(0, 2, half, 0)


def ratio(shares):
    counts = [len(share) for share in shares]
    parts = [x for share in shares for x in share]
    patches = parts[0].shape[0] // 12
    out = pl.pallas_call(
        functools.partial(ratio_kernel, counts),
        grid=(patches,),
        out_shape=jax.ShapeDtypeStruct((patches, FILTERS * 64, 256), F32),
        in_specs=[pl.BlockSpec((12, 16, 256), lambda i: (i, 0, 0))] * len(parts),
        out_specs=pl.BlockSpec((1, FILTERS * 64, 256), lambda i: (i, 0, 0)),
        scratch_shapes=[pltpu.VMEM((FILTERS * 64, 128), F32)],
        compiler_params=pltpu.CompilerParams(vmem_limit_bytes=48 * 2**20),
        name="ratio",
    )(*parts)
    return out.reshape(patches, FILTERS, 64, 256)


def tap_tables(kernel_x, kernel_y):
    jx = jnp.arange(48)[:, None]
    ix = jnp.arange(16)[None, :]
    pick = ((jx - ix - 6)[None] == jnp.arange(TAPS)[:, None, None]).astype(BF16)
    band_x = jnp.einsum("kt,tji->jki", kernel_x, pick, preferred_element_type=F32)
    band_x = band_x.astype(BF16).reshape(48, BASIS * 16)
    line = jnp.arange(512)
    tap = jnp.arange(TAPS)
    pick_y = (41 - (line // 16 + 16)[None, :] == tap[:, None]).astype(BF16)
    taps_y = jnp.dot(kernel_y, pick_y, preferred_element_type=F32).astype(BF16)
    row = jnp.arange(BASIS * 16)
    spread = (row[:, None] // 16 == jnp.arange(BASIS)[None, :]).astype(BF16)
    rows_y = jnp.dot(spread, taps_y, preferred_element_type=F32)
    rows_y = jnp.where(row[:, None] % 16 == line[None, :] % 16, rows_y, 0.0)
    return band_x, rows_y


def exchange(planes, groups):
    moved = [planes[0]]
    for s in range(1, groups):
        ring = [(i, (i + s) % groups) for i in range(groups)]
        moved.append(lax.ppermute(planes[s], "exp", ring))
    return moved


def on_device(images, variance, kernel_x, kernel_y, coef, exposure_filter, block_patch, patch_home):
    cell_count = images.shape[0]
    owner_count = lax.axis_size("patch")
    patches_local = patch_home.shape[0] // owner_count
    block_count = cell_count * 16

    targets = block_patch.reshape(-1)
    patch_index = targets // 4
    quadrant = targets % 4
    home_slot = jnp.sum(
        jnp.where(
            patch_index[:, None] == jnp.arange(patch_home.shape[0])[None, :], patch_home[None, :], 0
        ),
        axis=1,
    )
    owner_index = home_slot // patches_local
    local_patch = home_slot % patches_local
    band_index = jnp.repeat(exposure_filter, 16)
    order = jnp.arange(block_count)
    earlier = order[None, :] < order[:, None]
    rank = jnp.sum((owner_index[:, None] == owner_index[None, :]) & earlier, axis=1)
    late = rank >= CAP
    late_rank = jnp.sum(late[None, :] & earlier, axis=1)
    loose = late & (late_rank < LOOSE)
    more = jnp.any(late & (late_rank >= LOOSE))
    which = loose & (late_rank == jnp.arange(LOOSE)[:, None])
    which = jnp.max(jnp.where(which, order, -16), axis=1)
    dest = jnp.concatenate([owner_index * 8 + rank, which]).astype(jnp.int32)
    code = (
        (quadrant // 2) * 48 + (local_patch * 2 + quadrant % 2) * FILTERS + band_index
    )
    place = jnp.where(loose, ALL + late_rank, -1)
    more_place = jnp.where(late & ~loose, rank, -1)
    owners = jnp.arange(owner_count)[:, None, None]
    row = jnp.arange(16)[:, None]
    here = (rank == row) | (place == row) | (more_place + 5 == row) & (row >= 9)
    codes = jnp.min(jnp.where((owner_index == owners) & here, code, NONE), axis=2)
    codes = jnp.where(jnp.arange(16) == 8, more.astype(code.dtype), codes)
    codes = jnp.pad(codes.astype(BF16)[:, None, :], ((0, 0), (0, 15), (0, 240)))

    band_x, rows_y = tap_tables(kernel_x, kernel_y)
    coef_rows = jnp.repeat(coef, 16, axis=1)[:, :, None]
    free, mains, extras = match_cells(dest, images, variance, coef_rows, band_x, rows_y, codes)

    groups = lax.axis_size("exp")
    def send(part):
        return lax.all_to_all(part, "patch", 0, 0, tiled=True)

    gathered = lax.all_gather(free.reshape(-1, 256), "patch")
    got_0 = send(mains[0])
    head = got_0[:, ALL * 32, :16].astype(jnp.int32)
    got_code = head[:, :8].reshape(-1)
    group = jnp.stack([lax.axis_index("exp"), jnp.max(head[:, 8])])

    def add(got, c):
        return add_slots(got_code, group, got, 0, gathered, c - 1)

    hold = lax.optimization_barrier
    planes_0 = add_slots(got_code, group, got_0, 0)
    share_0 = exchange(planes_0, groups)
    got_1 = send(mains[1])
    part_2, own = hold((mains[2], planes_0[0]))
    share_0[0] = own
    planes_1 = add(got_1, 1)
    share_1 = exchange(planes_1, groups)
    got_2 = send(part_2)
    part_3, share_0, share_1[0] = hold((mains[3], share_0, share_1[0]))
    share_2 = exchange(add(got_2, 2), groups)
    got_3, share_1 = hold((send(part_3), share_1))
    share_3 = exchange(add(got_3, 3), groups)
    shares = [share_0, share_1, share_2, share_3]

    def plain(shares, extras, head):
        return ratio(shares)

    def with_more(shares, extras, head):
        codes = jnp.concatenate([head[:, :CAP], head[:, 9 : 9 + EXTRA], head[:, :2]], axis=1)
        parts = [shares[0]]
        for share, extra in zip(shares[1:], extras, strict=True):
            planes = add_slots(codes.reshape(-1), group, send(extra), CAP)
            parts.append([*share, *exchange(planes, groups)])
        return ratio(parts)

    more = functools.reduce(jnp.maximum, [x[48, 0, 0] for x in share_0]) > 0
    return lax.cond(more, with_more, plain, shares, extras, head)


def solution(mesh):
    return jax.shard_map(
        on_device,
        mesh=mesh,
        in_specs=(
            P(("exp", "patch"), None, None),
            P(("exp", "patch"), None, None),
            P(),
            P(),
            P(("exp", "patch"), None),
            P(("exp", "patch")),
            P(("exp", "patch"), None),
            P(),
        ),
        out_specs=P("patch", None, "exp", None),
        check_vma=False,
    )
```
